256 devices in a mesh: ctx: 32 (over y, x, core), mp: 8 (over z).
Axes of the slice: x: 4, y: 4, z: 8, core: 2. Of those that a mesh axis runs over, the one named last changes fastest.
Arguments:
- clip_store: bfloat16 [64, 512, 5120], P('ctx', None, 'mp'), may hold values from -96 to 96
- text_tokens: bfloat16 [4, 512, 5120], P(None, 'ctx', 'mp'), may hold values from -96 to 96
- candidates: int32 [4, 4], replicated, may hold values from 0 to 63, as said below
- clip_slot: int32 [64], replicated, may hold values from 0 to 63, as said below
- text_positions: int32 [4, 512], replicated, may hold values from 2048 to 2814, as said below
- block_order: int32 [64], replicated, may hold values from 0 to 63, as said below
- w_query: bfloat16 [5120, 5120], P(None, 'mp'), may hold values from -0.078125 to 0.078125
- b_query: bfloat16 [5120], P('mp'), may hold values from -6 to 6
- key_value_weight: bfloat16 [5120, 2, 1024], P(None, None, 'mp'), may hold values from -0.078125 to 0.078125
- value_offset_bias: bfloat16 [1024], P('mp'), may hold values from -3 to 3
Outputs:
- attended: bfloat16 [4, 64, 40, 5120], P(None, 'ctx', None, 'mp')
The draws below stay inside these ranges and needn't reach their ends.
Inputs may be any that keep to these rules, and one draw needn't show every extreme that they name: `candidates`: the 16 candidate clips lie on distinct store shards: the values clip_slot[c] // 2 differ for all of them. `clip_slot`: a permutation of the store rows. `text_positions`: along each query's text tokens the positions rise by 1 or 2 from 2048. `block_order`: a permutation; slots 2 i and 2 i + 1 hold blocks c and 63 - c for some c.
All inputs are finite; a program needn't handle non-finite values.
Results may differ from the reference program's by a relative error of at most 0.017.
The reference program's roundings to bfloat16 on the way count: a program that leaves them out, or rounds other values in their place, can miss the bound.
Values may be sent and summed in bfloat16 or wider, within the bound.
No kernel may reach another device: no remote copies, remote signals or barrier semaphores. Data moves between devices by JAX's collectives and lax.ppermute only.
A program may use at most 64 MiB of HBM per device.

```python
import jax
import jax.numpy as jnp
from jax import lax

EMBED_WIDTH = 5120
QUERY_HEADS = 40
KEY_VALUE_HEADS = 8
HEAD_SIZE = 128
CLIP_LEN = 512
TEXT_LEN = 512
CANDS = 4
CLIPS_DEV = 2
BATCH_QUERIES = 4
NUM_CLIPS = 64
CONTEXT_LENGTH = 2560
BLOCKS = 64
BLK = 40


def spread_values(key, array_shape, upper):
    value_rows = jnp.clip(jax.random.normal(jax.random.fold_in(key, 1), array_shape, jnp.float32), -6.0, 6.0)
    power = jax.random.uniform(jax.random.fold_in(key, 2), array_shape[:-1] + (1,), jnp.float32)
    row_scale = upper ** power
    return value_rows * row_scale


def draw_clip_store(key, part):
    key = jax.random.fold_in(key, 3)
    array_shape = (NUM_CLIPS, CLIP_LEN, EMBED_WIDTH)
    return spread_values(key, array_shape, 1.0).astype(jnp.bfloat16)


def draw_text_tokens(key, part):
    key = jax.random.fold_in(key, 4)
    array_shape = (BATCH_QUERIES, TEXT_LEN, EMBED_WIDTH)
    return spread_values(key, array_shape, 1.0).astype(jnp.bfloat16)


def pick_clips(key):
    permuted = jax.random.permutation(jax.random.fold_in(key, 11), NUM_CLIPS).astype(jnp.int32)
    shard_count = NUM_CLIPS // CLIPS_DEV
    pick_count = BATCH_QUERIES * CANDS
    last_slot = permuted[NUM_CLIPS - 1]
    last_shard = last_slot // CLIPS_DEV
    shard_keys = jax.random.permutation(jax.random.fold_in(key, 12), shard_count).astype(jnp.int32)
    shard_keys = jnp.where(jnp.arange(shard_count, dtype=jnp.int32) == last_shard, -1, shard_keys)
    chosen = jnp.argsort(shard_keys, stable=True)[:pick_count].astype(jnp.int32)
    offsets = jax.random.randint(jax.random.fold_in(key, 13), (pick_count,), 0, CLIPS_DEV, dtype=jnp.int32)
    offsets = offsets.at[0].set(last_slot % CLIPS_DEV)
    inverse = jnp.argsort(permuted).astype(jnp.int32)
    picked = jnp.take(inverse, chosen * CLIPS_DEV + offsets)
    placing = jax.random.permutation(jax.random.fold_in(key, 14), pick_count).astype(jnp.int32)
    picked = jnp.take(picked, placing)
    return (permuted, picked.reshape(BATCH_QUERIES, CANDS).astype(jnp.int32))


def draw_candidates(key, part):
    table, picked = pick_clips(key)
    return picked


def draw_clip_slot(key, part):
    table, picked = pick_clips(key)
    return table


def draw_text_positions(key, part):
    key = jax.random.fold_in(key, 7)
    seq_keys = jax.random.split(key, BATCH_QUERIES)

    def one_query(seq_key):
        permuted = jax.random.permutation(seq_key, TEXT_LEN - 1).astype(jnp.int32)
        increments = 1 + (permuted < (TEXT_LEN - 1) // 2).astype(jnp.int32)
        rising = jnp.concatenate([jnp.zeros((1,), jnp.int32), jnp.cumsum(increments).astype(jnp.int32)])
        return CANDS * CLIP_LEN + rising
    return jax.vmap(one_query)(seq_keys).astype(jnp.int32)


def draw_block_order(key, part):
    key = jax.random.fold_in(key, 5)
    half_count = BLOCKS // 2
    pair_ids = jax.random.permutation(jax.random.fold_in(key, 1), half_count).astype(jnp.int32)
    flipped = jax.random.randint(jax.random.fold_in(key, 2), (half_count,), 0, 2, dtype=jnp.int32)
    first_half = jnp.where(flipped == 1, BLOCKS - 1 - pair_ids, pair_ids)
    second = BLOCKS - 1 - first_half
    return jnp.stack([first_half, second], axis=1).reshape(BLOCKS).astype(jnp.int32)


def block_scale(rng, dims, pieces, smallest, top_value):
    def one(axis_at, shards_of):
        steps = jax.random.uniform(jax.random.fold_in(jax.random.fold_in(rng, 6), axis_at), (shards_of,), jnp.float32, smallest / len(pieces), top_value / len(pieces))
        return jnp.repeat(jnp.exp(steps), dims[axis_at] // shards_of).reshape((-1,) + (1,) * (len(dims) - axis_at - 1))

    gain = one(*pieces[0])
    for cut in pieces[1:]:
        gain = gain * one(*cut)
    return gain


def normal_values(key, shape, scale, most, cuts=(), kind=jnp.bfloat16):
    array = jax.random.normal(key, shape, jnp.float32) * scale
    if len(cuts) > 0:
        array = block_scale(key, shape, cuts, -0.22, 0.18) * array
    return jnp.clip(array, min=-most, max=most).astype(kind)


def setup_inputs(seed: int = 0) -> dict:
    key_of = jax.random.split(jax.random.key(seed), 11)
    return {
        "clip_store": draw_clip_store(jax.random.fold_in(key_of[10], 71), 0),
        "text_tokens": draw_text_tokens(jax.random.fold_in(key_of[10], 71), 0),
        "candidates": draw_candidates(jax.random.fold_in(key_of[10], 71), 0),
        "clip_slot": draw_clip_slot(jax.random.fold_in(key_of[10], 71), 0),
        "text_positions": draw_text_positions(jax.random.fold_in(key_of[10], 71), 0),
        "block_order": draw_block_order(jax.random.fold_in(key_of[10], 71), 0),
        "w_query": normal_values(key_of[6], (EMBED_WIDTH, QUERY_HEADS * HEAD_SIZE), EMBED_WIDTH ** -0.5, 0.078125, ((1, 8),)),
        "b_query": normal_values(key_of[7], (QUERY_HEADS * HEAD_SIZE,), 1.0, 6.0, ((0, 8),)),
        "key_value_weight": normal_values(key_of[8], (EMBED_WIDTH, 2, KEY_VALUE_HEADS * HEAD_SIZE), EMBED_WIDTH ** -0.5, 0.078125, ((2, 8),)),
        "value_offset_bias": normal_values(key_of[9], (KEY_VALUE_HEADS * HEAD_SIZE,), 0.5, 3.0, ((0, 8),)),
    }


NEG_FILL = -1e30
ROPE_BASE = 1000000.0


def apply_rotation(value_rows, positions, head_dim):
    half_dim = head_dim // 2
    frequency = ROPE_BASE ** (-(jnp.arange(half_dim, dtype=jnp.float32) * 2.0) / head_dim)
    angles = positions.astype(jnp.float32)[..., None] * frequency
    angles = jnp.concatenate([angles, angles], axis=-1)
    cosine = jnp.cos(angles)[..., None, :]
    sine_table = jnp.sin(angles)[..., None, :]
    first_half = value_rows[..., :half_dim]
    second = value_rows[..., half_dim:]
    turned = jnp.concatenate([-second, first_half], axis=-1)
    return value_rows * cosine + turned * sine_table


def reference(clip_store, text_tokens, candidates, clip_slot, text_positions, block_order, w_query, b_query, key_value_weight, value_offset_bias):
    store_slots = jnp.take(clip_slot, candidates.reshape(-1))
    visual = jnp.take(clip_store, store_slots, axis=0).reshape(BATCH_QUERIES, CANDS * CLIP_LEN, EMBED_WIDTH)
    context = jnp.concatenate([visual, text_tokens], axis=1)
    flattened_rows = context.reshape(BATCH_QUERIES * CONTEXT_LENGTH, EMBED_WIDTH)
    query_raw = jnp.dot(flattened_rows, w_query, preferred_element_type=jnp.float32) + b_query.astype(jnp.float32)
    key_value_pairs = jnp.dot(flattened_rows, key_value_weight.reshape(EMBED_WIDTH, 2 * KEY_VALUE_HEADS * HEAD_SIZE), preferred_element_type=jnp.float32)
    unrotated_key = key_value_pairs[:, :KEY_VALUE_HEADS * HEAD_SIZE]
    value_rows = (key_value_pairs[:, KEY_VALUE_HEADS * HEAD_SIZE:] + value_offset_bias.astype(jnp.float32)).astype(jnp.bfloat16).reshape(BATCH_QUERIES, CONTEXT_LENGTH, KEY_VALUE_HEADS, HEAD_SIZE)
    visual_pos = jnp.broadcast_to(jnp.arange(CANDS * CLIP_LEN, dtype=jnp.int32)[None, :], (BATCH_QUERIES, CANDS * CLIP_LEN))
    rotary_positions = jnp.concatenate([visual_pos, text_positions.astype(jnp.int32)], axis=1)
    query_vectors = apply_rotation(query_raw.reshape(BATCH_QUERIES, CONTEXT_LENGTH, QUERY_HEADS, HEAD_SIZE), rotary_positions, HEAD_SIZE).astype(jnp.bfloat16)
    rotated_key_rows = apply_rotation(unrotated_key.reshape(BATCH_QUERIES, CONTEXT_LENGTH, KEY_VALUE_HEADS, HEAD_SIZE), rotary_positions, HEAD_SIZE).astype(jnp.bfloat16)
    heads_per_group = QUERY_HEADS // KEY_VALUE_HEADS
    grouped_heads = query_vectors.reshape(BATCH_QUERIES, CONTEXT_LENGTH, KEY_VALUE_HEADS, heads_per_group, HEAD_SIZE)
    causal = jnp.arange(CONTEXT_LENGTH, dtype=jnp.int32)[None, :] <= jnp.arange(CONTEXT_LENGTH, dtype=jnp.int32)[:, None]
    score_scale = 1.0 / (HEAD_SIZE ** 0.5)

    def single_head(entry_number):
        sequence_number = entry_number // KEY_VALUE_HEADS
        head_number = entry_number % KEY_VALUE_HEADS
        query_seq = lax.dynamic_index_in_dim(grouped_heads, sequence_number, 0, keepdims=False)
        query_block = lax.dynamic_index_in_dim(query_seq, head_number, 1, keepdims=False).astype(jnp.float32)
        key_seq = lax.dynamic_index_in_dim(rotated_key_rows, sequence_number, 0, keepdims=False)
        key_block = lax.dynamic_index_in_dim(key_seq, head_number, 1, keepdims=False).astype(jnp.float32)
        value_seq = lax.dynamic_index_in_dim(value_rows, sequence_number, 0, keepdims=False)
        value_block = lax.dynamic_index_in_dim(value_seq, head_number, 1, keepdims=False).astype(jnp.float32)
        scores = jnp.einsum("qgd,nd->gqn", query_block, key_block) * score_scale
        scores = jnp.where(causal[None], scores, NEG_FILL)
        row_max = jnp.max(scores, axis=-1, keepdims=True)
        weights = jnp.where(causal[None], jnp.exp(scores - row_max), 0.0)
        row_sum = jnp.sum(weights, axis=-1)
        rounded = lax.optimization_barrier(weights.astype(jnp.bfloat16)).astype(jnp.float32)
        return jnp.einsum("gqn,nd->gqd", rounded, value_block) / row_sum[..., None]

    head_outputs = lax.map(single_head, jnp.arange(BATCH_QUERIES * KEY_VALUE_HEADS, dtype=jnp.int32))
    head_outputs = head_outputs.reshape(BATCH_QUERIES, KEY_VALUE_HEADS, heads_per_group, CONTEXT_LENGTH, HEAD_SIZE)
    head_outputs = jnp.transpose(head_outputs, (0, 3, 1, 2, 4)).reshape(BATCH_QUERIES, CONTEXT_LENGTH, QUERY_HEADS * HEAD_SIZE).astype(jnp.bfloat16)
    blocked = head_outputs.reshape(BATCH_QUERIES, BLOCKS, BLK, QUERY_HEADS * HEAD_SIZE)
    return jnp.take(blocked, block_order.astype(jnp.int32), axis=1)
```

```python
import functools
import math

import jax
import jax.numpy as jnp
from jax import lax
from jax.experimental import pallas as pl
from jax.experimental.pallas import tpu as pltpu
from jax.sharding import PartitionSpec as P

HEAD = 128
NEG_FILL = -1e30
ROPE_BASE = 1000000.0
GROUPS = 4
MEMBERS = 8
PLANES = 8


def shifted(n, by):
    return [(i, (i + by) % n) for i in range(n)]


def ctx_pairs(dy=0, dx=0, dc=0):
    pairs = []
    for i in range(32):
        y, x, c = i // 8, (i // 2) % 4, i % 2
        pairs.append((i, ((y + dy) % 4) * 8 + ((x + dx) % 4) * 2 + (c + dc) % 2))
    return pairs


def rope_tables(positions):
    half = HEAD // 2
    frequency = ROPE_BASE ** (-(jnp.arange(half, dtype=jnp.float32) * 2.0) / HEAD)
    angles = positions.astype(jnp.float32)[:, None] * frequency
    angles = jnp.concatenate([angles, angles], axis=-1)
    return jnp.cos(angles), jnp.sin(angles)


def rotate(rows, cosine, sine):
    half = HEAD // 2
    turned = jnp.concatenate([-rows[..., half:], rows[..., :half]], axis=-1)
    return rows * cosine[:, None, :] + turned * sine[:, None, :]


def attend_kernel(heads, step, first, last, member_ref, q_ref, k_ref, v_ref, o_ref):
    member = member_ref[0]
    keys_step = MEMBERS * step
    scale = 1.0 / math.sqrt(HEAD)
    shape = (heads, step, MEMBERS, step)
    q_idx = lax.broadcasted_iota(jnp.int32, (step, keys_step), 0)
    lane = lax.broadcasted_iota(jnp.int32, (step, keys_step), 1)
    k_idx = lane % step
    k_mem = lane // step
    allowed = (k_idx < q_idx) | ((k_idx == q_idx) & (k_mem <= member))
    allowed = jnp.concatenate([allowed] * heads, axis=0)
    for part in range(first, last):
        rows = pl.ds((part - first) * step, step)
        q = jnp.concatenate(
            [q_ref[rows, h * HEAD : (h + 1) * HEAD] for h in range(heads)], axis=0
        )
        scores = []
        for kp in range(part + 1):
            keys = k_ref[:, kp * step : (kp + 1) * step, :].reshape(keys_step, HEAD)
            s = lax.dot_general(
                q, keys, (((1,), (1,)), ((), ())), preferred_element_type=jnp.float32
            ) * scale
            if kp == part:
                s = jnp.where(allowed, s, NEG_FILL)
            scores.append(s)
        top = functools.reduce(
            jnp.maximum, [jnp.max(s, axis=-1, keepdims=True) for s in scores]
        )
        total = jnp.zeros((heads * step, 1), jnp.float32)
        acc = jnp.zeros((heads * step, HEAD), jnp.float32)
        for kp, s in enumerate(scores):
            w = jnp.exp(s - top)
            total = total + jnp.sum(w, axis=-1, keepdims=True)
            vals = v_ref[:, kp * step : (kp + 1) * step, :].reshape(keys_step, HEAD)
            acc = acc + jnp.dot(
                w.astype(jnp.bfloat16), vals, preferred_element_type=jnp.float32
            )
        out = (acc / total).astype(jnp.bfloat16)
        for h in range(heads):
            o_ref[rows, h * HEAD : (h + 1) * HEAD] = out[h * step : (h + 1) * step, :]


def attend(member, q, k, v, heads, step, first, last):
    vmem = pl.BlockSpec(memory_space=pltpu.VMEM)
    return pl.pallas_call(
        functools.partial(attend_kernel, heads, step, first, last),
        out_shape=jax.ShapeDtypeStruct(q.shape, jnp.bfloat16),
        in_specs=[pl.BlockSpec(memory_space=pltpu.SMEM), vmem, vmem, vmem],
        out_specs=vmem,
        compiler_params=pltpu.CompilerParams(vmem_limit_bytes=48 * 1024 * 1024),
        cost_estimate=pl.CostEstimate(
            flops=1300000000, bytes_accessed=4000000, transcendentals=2500000
        ),
    )(member, q, k, v)


def per_device(
    clip_store,
    text_tokens,
    candidates,
    clip_slot,
    text_positions,
    block_order,
    w_query,
    b_query,
    key_value_weight,
    value_offset_bias,
):
    me = lax.axis_index("ctx")
    plane = lax.axis_index("mp")
    group = me // MEMBERS
    member = me % MEMBERS
    clips_here, clip_len, feat = clip_store.shape
    seqs, cands = candidates.shape
    text_len = text_positions.shape[1]
    devices = GROUPS * MEMBERS
    per = clip_len // devices
    text_here = text_tokens.shape[1]

    slots = jnp.take(clip_slot, candidates.reshape(-1))
    holders = slots // clips_here
    which = jnp.sum(jnp.where(holders == me, slots % clips_here, 0))
    held = lax.dynamic_index_in_dim(clip_store, which, 0, keepdims=False)
    held = held.reshape(GROUPS, per, MEMBERS, feat).transpose(0, 2, 1, 3)
    held = held.reshape(devices, per, feat)
    texts = text_tokens.reshape(seqs, text_here // MEMBERS, MEMBERS, feat)
    texts = texts.transpose(0, 2, 1, 3).reshape(devices, text_here // MEMBERS, feat)
    sent = jnp.concatenate([held, texts], axis=1)
    sent = lax.all_to_all(sent, "ctx", 0, 0, tiled=True)
    got = jnp.take(sent[:, :per], holders, axis=0).reshape(seqs, cands, per, feat)
    text_rows = sent[:, per:].reshape(-1, feat)

    pieces = []
    for dy in range(GROUPS):
        seq_to = (group + dy) % GROUPS
        out = lax.dynamic_index_in_dim(got, seq_to, 0, keepdims=False)
        pieces.append(out if dy == 0 else lax.ppermute(out, "ctx", ctx_pairs(dy=dy)))
    stacked = jnp.stack(pieces, axis=0)
    order = (group - jnp.arange(GROUPS)) % GROUPS
    stacked = jnp.take(stacked, order, axis=0)
    rows = jnp.transpose(stacked, (1, 0, 2, 3)).reshape(-1, feat)
    rows = jnp.concatenate([rows, text_rows], axis=0)
    count = rows.shape[0]

    width = w_query.shape[1]
    kv_flat = key_value_weight.reshape(key_value_weight.shape[0], -1)

    def product(part, owner):
        wq = lax.dynamic_slice_in_dim(w_query, owner * feat, feat, 0)
        wk = lax.dynamic_slice_in_dim(kv_flat, owner * feat, feat, 0)
        return (
            jnp.dot(part, wq, preferred_element_type=jnp.float32),
            jnp.dot(part, wk, preferred_element_type=jnp.float32),
        )

    def add(a, b):
        return (a[0] + b[0], a[1] + b[1])

    sums = product(rows, plane)
    fwd, bwd = rows, rows
    for hop in range(1, PLANES // 2):
        fwd = lax.ppermute(fwd, "mp", shifted(PLANES, 1))
        bwd = lax.ppermute(bwd, "mp", shifted(PLANES, -1))
        sums = add(sums, product(fwd, (plane - hop) % PLANES))
        sums = add(sums, product(bwd, (plane + hop) % PLANES))
    cut = count // 2
    far = jnp.concatenate(
        [
            lax.ppermute(fwd[:cut], "mp", shifted(PLANES, 1)),
            lax.ppermute(bwd[cut:], "mp", shifted(PLANES, -1)),
        ],
        axis=0,
    )
    q_sum, kv_sum = add(sums, product(far, (plane + PLANES // 2) % PLANES))

    visual = cands * clip_len
    pos = MEMBERS * jnp.arange(count, dtype=jnp.int32) + member
    my_text = lax.dynamic_index_in_dim(text_positions, group, 0, keepdims=False)
    text_at = lax.dynamic_index_in_dim(
        my_text.reshape(text_len // MEMBERS, MEMBERS), member, 1, keepdims=False
    )
    rope_pos = jnp.concatenate([pos[: visual // MEMBERS], text_at], axis=0)
    cosine, sine = rope_tables(rope_pos)
    heads = width // HEAD
    q_raw = (q_sum + b_query.astype(jnp.float32)).reshape(count, heads, HEAD)
    queries = rotate(q_raw, cosine, sine).astype(jnp.bfloat16).reshape(count, width)
    k_raw = kv_sum[:, :HEAD].reshape(count, 1, HEAD)
    keys = rotate(k_raw, cosine, sine).astype(jnp.bfloat16).reshape(count, HEAD)
    values = (kv_sum[:, HEAD:] + value_offset_bias.astype(jnp.float32)).astype(jnp.bfloat16)

    own = jnp.stack([keys, values], axis=0)
    by_x = [own] + [lax.ppermute(own, "ctx", ctx_pairs(dx=dx)) for dx in range(1, 4)]
    by_x = jnp.stack(by_x, axis=0)
    my_x, my_core = member // 2, member % 2
    by_x = jnp.take(by_x, (my_x - jnp.arange(4)) % 4, axis=0)
    other = lax.ppermute(by_x, "ctx", ctx_pairs(dc=1))
    both = jnp.where(my_core == 0, jnp.stack([by_x, other], 1), jnp.stack([other, by_x], 1))
    both = both.reshape(MEMBERS, 2, count, HEAD)
    all_keys, all_values = both[:, 0], both[:, 1]

    out = attend(
        member.astype(jnp.int32).reshape(1), queries, all_keys, all_values,
        heads, clip_len // MEMBERS, 0, count * MEMBERS // clip_len,
    )

    blocks = block_order.shape[0]
    block_len = (visual + text_len) // blocks
    sub = block_len // MEMBERS
    send = jnp.take(out.reshape(blocks, sub, width), block_order, axis=0)
    send = send.reshape(devices, 2 * sub, width)
    recv = lax.all_to_all(send, "ctx", 0, 0, tiled=True)
    recv = recv.reshape(GROUPS, MEMBERS, 2, sub, width)
    return recv.transpose(0, 2, 3, 1, 4).reshape(seqs, 2, block_len, width)


def solution(mesh):
    placed = (
        P("ctx", None, "mp"),
        P(None, "ctx", "mp"),
        P(),
        P(),
        P(),
        P(),
        P(None, "mp"),
        P("mp"),
        P(None, None, "mp"),
        P("mp"),
    )
    return jax.shard_map(
        per_device,
        mesh=mesh,
        in_specs=placed,
        out_specs=P(None, "ctx", None, "mp"),
        check_vma=False,
    )
```

```python
import functools
import math

import jax
import jax.numpy as jnp
from jax import lax
from jax.experimental import pallas as pl
from jax.experimental.pallas import tpu as pltpu
from jax.sharding import PartitionSpec as P

HEAD = 128
NEG_FILL = -1e30
ROPE_BASE = 1000000.0
GROUPS = 4
MEMBERS = 8
DEVICES = GROUPS * MEMBERS
PLANES = 8
MULTIPLY_AT = (1, 2, 3)
STEP = 64
PART = 16
TEXT = 2
SMALL_VMEM = 16 * 1024 * 1024
MID_VMEM = 24 * 1024 * 1024
VMEM_SPEC = pl.BlockSpec(memory_space=pltpu.VMEM)
SMEM_SPEC = pl.BlockSpec(memory_space=pltpu.SMEM)
HBM_SPEC = pl.BlockSpec(memory_space=pltpu.HBM)


def in_hbm(*arrays):
    return [pltpu.with_memory_space_constraint(array, pltpu.HBM) for array in arrays]


def shifted(n, by):
    return [(i, (i + by) % n) for i in range(n)]


def ctx_pairs(move):
    pairs = []
    for i in range(DEVICES):
        y, x, c = move(i // MEMBERS, (i // 2) % 4, i % 2)
        pairs.append((i, (y % 4) * MEMBERS + (x % 4) * 2 + c))
    return pairs


def across(first):
    return ctx_pairs(lambda y, x, c: (y, x ^ (1 if (c == 0) == first else 3), c))


def far_pairs():
    return [
        (i * PLANES + z, i * PLANES + (z + (1 if i % 2 == 0 else -1)) % PLANES)
        for i in range(DEVICES)
        for z in range(PLANES)
    ]


def rope_tables(positions):
    half = HEAD // 2
    frequency = ROPE_BASE ** (-(jnp.arange(half, dtype=jnp.float32) * 2.0) / HEAD)
    angles = positions.astype(jnp.float32)[:, None] * frequency
    cosine, sine = jnp.cos(angles), jnp.sin(angles)
    return jnp.concatenate([cosine, cosine], -1), jnp.concatenate([-sine, sine], -1)


def rows_of(refs):
    return refs[0][...] if len(refs) == 1 else jnp.concatenate([r[...] for r in refs], axis=0)


def products_kernel(groups, halves, fresh, owners_ref, wq_hbm, wk_hbm, *refs):
    wq_ref, wk_ref, sems = refs[-3:]
    q_out, k_out = refs[-5:-3]
    feat = wq_ref.shape[1]
    copies = []
    for i in range(groups):
        at = pl.ds(pl.multiple_of(owners_ref[i] * feat, feat), feat)
        for n, (src, dst) in enumerate(((wq_hbm, wq_ref), (wk_hbm, wk_ref))):
            copy = pltpu.make_async_copy(src.at[at, :], dst.at[i], sems.at[n, i])
            copy.start()
            copies.append(copy)
    q = None if fresh else refs[-7][...]
    k = None if fresh else refs[-6][...]
    for i in range(groups):
        copies[2 * i].wait()
        copies[2 * i + 1].wait()
        rows = rows_of(refs[i * halves : (i + 1) * halves])
        more_q = jnp.dot(rows, wq_ref[i], preferred_element_type=jnp.float32)
        more_k = jnp.dot(rows, wk_ref[i], preferred_element_type=jnp.float32)
        q = more_q if q is None else q + more_q
        k = more_k if k is None else k + more_k
    q_out[...] = q
    k_out[...] = k


def add_products(sums, parts, owners, w_query, kv_flat):
    halves, groups = len(parts[0]), len(parts)
    feat = parts[0][0].shape[1]
    count = sum(part.shape[0] for part in parts[0])
    q_cols, k_cols = w_query.shape[1], kv_flat.shape[1]
    args = sum(parts, []) + list(sums or ())
    return pl.pallas_call(
        functools.partial(products_kernel, groups, halves, sums is None),
        in_specs=[SMEM_SPEC, HBM_SPEC, HBM_SPEC] + [VMEM_SPEC] * len(args),
        out_specs=[VMEM_SPEC] * 2,
        out_shape=[
            jax.ShapeDtypeStruct((count, q_cols), jnp.float32),
            jax.ShapeDtypeStruct((count, k_cols), jnp.float32),
        ],
        scratch_shapes=[
            pltpu.VMEM((groups, feat, q_cols), jnp.bfloat16),
            pltpu.VMEM((groups, feat, k_cols), jnp.bfloat16),
            pltpu.SemaphoreType.DMA((2, groups)),
        ],
        compiler_params=pltpu.CompilerParams(vmem_limit_bytes=SMALL_VMEM),
        cost_estimate=pl.CostEstimate(
            flops=4 * groups * count * feat * (q_cols + k_cols),
            bytes_accessed=groups * feat * (q_cols + k_cols) * 2,
            transcendentals=0,
        ),
    )(jnp.stack(owners).astype(jnp.int32), *in_hbm(w_query, kv_flat), *args)


def finish_kernel(halves, owner_ref, wq_hbm, wk_hbm, *refs):
    q_sum, k_sum, cos_ref, sin_ref, qb_ref, vb_ref, q_out, kv_out, wq_ref, wk_ref, sems = refs[halves:]
    feat = wq_ref.shape[0]
    at = pl.ds(pl.multiple_of(owner_ref[0] * feat, feat), feat)
    copy_k = pltpu.make_async_copy(wk_hbm.at[at, :], wk_ref, sems.at[0])
    copy_q = pltpu.make_async_copy(wq_hbm.at[at, :], wq_ref, sems.at[1])
    copy_k.start()
    copy_q.start()
    rows = rows_of(refs[:halves])
    copy_k.wait()
    k = k_sum[...] + jnp.dot(rows, wk_ref[...], preferred_element_type=jnp.float32)
    copy_q.wait()
    q = q_sum[...] + jnp.dot(rows, wq_ref[...], preferred_element_type=jnp.float32)
    q = q + qb_ref[...].astype(jnp.float32)
    cosine, sine = cos_ref[...], sin_ref[...]

    def rotated(x):
        return (x * cosine + pltpu.roll(x, HEAD // 2, 1) * sine).astype(jnp.bfloat16)

    kv_out[:, :HEAD] = rotated(k[:, :HEAD])
    kv_out[:, HEAD:] = (k[:, HEAD:] + vb_ref[...].astype(jnp.float32)).astype(jnp.bfloat16)
    for h in range(q.shape[1] // HEAD):
        at = slice(h * HEAD, (h + 1) * HEAD)
        q_out[:, at] = rotated(q[:, at])


def finish(sums, far, owner, w_query, kv_flat, cosine, sine, q_bias, v_bias):
    count, feat = sums[0].shape[0], far[0].shape[1]
    q_cols, k_cols = w_query.shape[1], kv_flat.shape[1]
    args = [*far, *sums, cosine, sine, q_bias.reshape(1, -1), v_bias.reshape(1, -1)]
    return pl.pallas_call(
        functools.partial(finish_kernel, len(far)),
        in_specs=[SMEM_SPEC, HBM_SPEC, HBM_SPEC] + [VMEM_SPEC] * len(args),
        out_specs=[VMEM_SPEC] * 2,
        out_shape=[jax.ShapeDtypeStruct(s.shape, jnp.bfloat16) for s in sums],
        scratch_shapes=[
            pltpu.VMEM((feat, q_cols), jnp.bfloat16),
            pltpu.VMEM((feat, k_cols), jnp.bfloat16),
            pltpu.SemaphoreType.DMA((2,)),
        ],
        compiler_params=pltpu.CompilerParams(vmem_limit_bytes=SMALL_VMEM),
        cost_estimate=pl.CostEstimate(
            flops=2 * count * feat * (q_cols + k_cols), bytes_accessed=2000000, transcendentals=0
        ),
    )(owner.reshape(1).astype(jnp.int32), *in_hbm(w_query, kv_flat), *args)


def one_hot(hit):
    return jnp.where(hit, 1.0, 0.0).astype(jnp.bfloat16)


def iotas(shape):
    return lax.broadcasted_iota(jnp.int32, shape, 0), lax.broadcasted_iota(jnp.int32, shape, 1)


def pack_kernel(clips_here, cand_ref, slot_ref, me_ref, clip_hbm, text_ref, o_ref, held_ref, sem):
    me = me_ref[0]
    which = jnp.int32(0)
    for s in range(cand_ref.shape[0]):
        for k in range(cand_ref.shape[1]):
            slot = slot_ref[cand_ref[s, k]]
            which = jnp.where(slot // clips_here == me, slot % clips_here, which)
    copy = pltpu.make_async_copy(clip_hbm.at[which], held_ref, sem)
    copy.start()
    feat = held_ref.shape[1]
    folds = feat // HEAD
    rows = PART * MEMBERS
    to, at = iotas((rows, PART))
    m, r = to // PART, to % PART
    for y in range(GROUPS):
        text = text_ref[y]
        beside = jnp.zeros((rows, HEAD), jnp.float32)
        for fold in range(folds):
            hit = (r % folds == fold) & (r < TEXT * folds) & (at == m + MEMBERS * (r // folds))
            beside = beside + jnp.dot(
                one_hot(hit), text[:, fold * HEAD : (fold + 1) * HEAD],
                preferred_element_type=jnp.float32,
            )
        o_ref[pl.ds(y * MEMBERS, MEMBERS), :, feat:] = beside.astype(jnp.bfloat16).reshape(
            MEMBERS, PART, HEAD
        )
    to, at = iotas((rows, rows))
    pick = one_hot(at == MEMBERS * (to % PART) + to // PART)
    copy.wait()
    for y in range(GROUPS):
        out = jnp.dot(pick, held_ref[rows * y : rows * (y + 1)], preferred_element_type=jnp.float32)
        o_ref[pl.ds(y * MEMBERS, MEMBERS), :, :feat] = out.astype(jnp.bfloat16).reshape(
            MEMBERS, PART, feat
        )


def pack(candidates, clip_slot, me, clip_store, text_tokens):
    clips_here, clip_len, feat = clip_store.shape
    return pl.pallas_call(
        functools.partial(pack_kernel, clips_here),
        out_shape=jax.ShapeDtypeStruct((DEVICES, PART, feat + HEAD), jnp.bfloat16),
        in_specs=[SMEM_SPEC] * 3 + [HBM_SPEC, VMEM_SPEC],
        out_specs=VMEM_SPEC,
        scratch_shapes=[pltpu.VMEM((clip_len, feat), jnp.bfloat16), pltpu.SemaphoreType.DMA],
        compiler_params=pltpu.CompilerParams(vmem_limit_bytes=SMALL_VMEM),
    )(*in_hbm(candidates, clip_slot), me.reshape(1).astype(jnp.int32), *in_hbm(clip_store, text_tokens))


def unpack_kernel(clips_here, cand_ref, slot_ref, group_ref, sent_ref, own_ref, *out_refs):
    group = group_ref[0]
    feat = own_ref.shape[1]
    folds = feat // HEAD
    beside = sent_ref[:, :, feat:].reshape(DEVICES * PART, HEAD)
    to, at = iotas((TEXT * DEVICES, DEVICES * PART))
    for fold in range(folds):
        hit = at == (to // TEXT) * PART + (to % TEXT) * folds + fold
        own_ref[:STEP, fold * HEAD : (fold + 1) * HEAD] = jnp.dot(
            one_hot(hit), beside, preferred_element_type=jnp.float32
        ).astype(jnp.bfloat16)
    cands = cand_ref.shape[1]
    for dy in range(GROUPS):
        seq = (group + dy) % GROUPS
        for k in range(cands):
            source = slot_ref[cand_ref[seq, k]] // clips_here
            rows = sent_ref[source, :, :feat]
            if dy == 0:
                own_ref[STEP + PART * k : STEP + PART * (k + 1)] = rows
            else:
                out_refs[dy - 1][PART * k : PART * (k + 1)] = rows


def unpack(candidates, clip_slot, group, sent, clips_here):
    feat = sent.shape[2] - HEAD
    shapes = [(2 * STEP, feat)] + [(STEP, feat)] * (GROUPS - 1)
    return pl.pallas_call(
        functools.partial(unpack_kernel, clips_here),
        out_shape=[jax.ShapeDtypeStruct(s, jnp.bfloat16) for s in shapes],
        in_specs=[SMEM_SPEC] * 3 + [VMEM_SPEC],
        out_specs=[VMEM_SPEC] * GROUPS,
        compiler_params=pltpu.CompilerParams(vmem_limit_bytes=SMALL_VMEM),
    )(*in_hbm(candidates, clip_slot), group.reshape(1).astype(jnp.int32), sent)


def attend_kernel(heads, clips, info_ref, q_ref, *refs):
    o_ref, key_refs = refs[-1], refs[:-1]
    group, member = info_ref[0], info_ref[1]
    my_x, my_core = member // 2, member % 2
    scale = math.log2(math.e) / math.sqrt(HEAD)

    def spans(part):
        if part == clips:
            return [(0, STEP)]
        return [(STEP + dy * STEP + PART * part, PART) for dy in range(GROUPS)]

    def idx_of(row, part):
        if part == clips:
            return row
        return ((group + GROUPS - row // PART) % GROUPS) * PART + row % PART

    keys_step = MEMBERS * STEP
    lane = lax.broadcasted_iota(jnp.int32, (STEP, keys_step), 1)
    row = lax.broadcasted_iota(jnp.int32, (STEP, keys_step), 0)
    slot = lane // STEP
    core = (my_core + slot // 4) % 2
    by_near, by_far = jnp.where(core == 0, 1, 3), jnp.where(core == 0, 3, 1)
    x = my_x ^ jnp.where(slot % 2 == 1, by_near, 0) ^ jnp.where((slot // 2) % 2 == 1, by_far, 0)
    k_mem = 2 * x + core

    def gather(part, at):
        return jnp.concatenate(
            [
                ref[piece, pl.ds(first, n), at : at + HEAD]
                for ref in key_refs
                for piece in range(2)
                for first, n in spans(part)
            ],
            axis=0,
        )

    for part in range(clips + 1):
        k_pos = MEMBERS * idx_of(lane % STEP, part) + k_mem
        q_pos = MEMBERS * idx_of(row, part) + member
        allowed = jnp.concatenate([k_pos <= q_pos] * heads, axis=0)
        q = jnp.concatenate(
            [
                q_ref[pl.ds(first, n), h * HEAD : (h + 1) * HEAD]
                for h in range(heads)
                for first, n in spans(part)
            ],
            axis=0,
        )
        scores = []
        for kp in range(part + 1):
            s = lax.dot_general(
                q, gather(kp, 0), (((1,), (1,)), ((), ())), preferred_element_type=jnp.float32
            ) * scale
            if kp == part:
                s = jnp.where(allowed, s, NEG_FILL)
            scores.append(s)
        top = functools.reduce(
            jnp.maximum, [jnp.max(s, axis=-1, keepdims=True) for s in scores]
        )
        total = jnp.zeros((heads * STEP, 1), jnp.float32)
        acc = jnp.zeros((heads * STEP, HEAD), jnp.float32)
        for kp, s in enumerate(scores):
            w = jnp.exp2(s - top)
            total = total + jnp.sum(w, axis=-1, keepdims=True)
            acc = acc + jnp.dot(
                w.astype(jnp.bfloat16), gather(kp, HEAD), preferred_element_type=jnp.float32
            )
        out = (acc / total).astype(jnp.bfloat16)
        for h in range(heads):
            at = slice(h * HEAD, (h + 1) * HEAD)
            if part == clips:
                o_ref[pl.ds(part * STEP, STEP), at] = out[h * STEP : (h + 1) * STEP]
                continue
            for dy in range(GROUPS):
                y = (group + GROUPS - dy) % GROUPS
                to = pl.ds(pl.multiple_of(part * STEP + y * PART, PART), PART)
                first = h * STEP + dy * PART
                o_ref[to, at] = out[first : first + PART]


def attend(info, q, pieces, heads, clips):
    return pl.pallas_call(
        functools.partial(attend_kernel, heads, clips),
        out_shape=jax.ShapeDtypeStruct(q.shape, jnp.bfloat16),
        in_specs=[SMEM_SPEC] + [VMEM_SPEC] * (1 + len(pieces)),
        out_specs=VMEM_SPEC,
        compiler_params=pltpu.CompilerParams(vmem_limit_bytes=MID_VMEM),
        cost_estimate=pl.CostEstimate(
            flops=1300000000, bytes_accessed=4000000, transcendentals=2500000
        ),
    )(info, q, *pieces)


def per_device(
    clip_store,
    text_tokens,
    candidates,
    clip_slot,
    text_positions,
    block_order,
    w_query,
    b_query,
    key_value_weight,
    value_offset_bias,
):
    me = lax.axis_index("ctx")
    plane = lax.axis_index("mp")
    group, member = me // MEMBERS, me % MEMBERS
    core = member % 2
    clips_here, clip_len, feat = clip_store.shape
    seqs, cands = candidates.shape
    text_len = text_positions.shape[1]
    width = w_query.shape[1]
    heads = width // HEAD

    sent = pack(candidates, clip_slot, me, clip_store, text_tokens)
    sent = lax.all_to_all(sent, "ctx", 0, 0, tiled=True)

    kv_flat = key_value_weight.reshape(key_value_weight.shape[0], -1)
    text_at = lax.dynamic_index_in_dim(
        lax.dynamic_index_in_dim(text_positions, group, 0, keepdims=False).reshape(-1, MEMBERS),
        member, 1, keepdims=False,
    )
    clip_idx = STEP * jnp.arange(cands)[:, None] + jnp.arange(PART)[None, :]

    def clip_pos(dy):
        y = (group - dy) % GROUPS
        return (MEMBERS * (clip_idx + PART * y) + member).astype(jnp.int32).reshape(-1)

    cosine, sine = rope_tables(jnp.concatenate([text_at] + [clip_pos(dy) for dy in range(GROUPS)]))
    sent, kv_flat, cosine, sine = lax.optimization_barrier((sent, kv_flat, cosine, sine))

    first, *others = unpack(candidates, clip_slot, group, sent, clips_here)
    arrived = [
        lax.ppermute(out, "ctx", ctx_pairs(lambda y, x, c, dy=dy: (y + dy, x, c)))
        for dy, out in enumerate(others, 1)
    ]
    own = [first, jnp.concatenate(arrived, 0)]

    fwd, bwd = list(own), list(own)
    sums, parts, owners = None, [own], [plane]
    for hop in range(1, PLANES // 2):
        for h in range(len(own)):
            fwd[h] = lax.ppermute(fwd[h], "mp", shifted(PLANES, 1))
            bwd[h] = lax.ppermute(bwd[h], "mp", shifted(PLANES, -1))
        if hop in MULTIPLY_AT:
            sums = add_products(sums, parts, owners, w_query, kv_flat)
            fwd[-1], bwd[-1], sums = lax.optimization_barrier((fwd[-1], bwd[-1], sums))
            parts, owners = [], []
        parts += [list(fwd), list(bwd)]
        owners += [(plane - hop) % PLANES, (plane + hop) % PLANES]
    far = [
        lax.ppermute(jnp.where(core == 0, fwd[h], bwd[h]), ("ctx", "mp"), far_pairs())
        for h in range(len(own))
    ]
    sums = add_products(sums, parts, owners, w_query, kv_flat)
    far[-1], sums = lax.optimization_barrier((far[-1], sums))
    q, kv = finish(
        sums, far, (plane + PLANES // 2) % PLANES, w_query, kv_flat,
        cosine, sine, b_query, value_offset_bias,
    )

    near = jnp.stack([kv, lax.ppermute(kv, "ctx", across(True))])
    off = lax.ppermute(near, "ctx", across(False))
    swap = ctx_pairs(lambda y, x, c: (y, x, 1 - c))
    pieces = [near, off, lax.ppermute(near, "ctx", swap), lax.ppermute(off, "ctx", swap)]

    info = jnp.stack([group, member]).astype(jnp.int32)
    out = attend(info, q, pieces, heads, cands)

    blocks = block_order.shape[0]
    block_len = (cands * clip_len + text_len) // blocks
    sub = block_len // MEMBERS
    send = jnp.take(out.reshape(blocks, sub, width), block_order, axis=0)
    send = send.reshape(DEVICES, 2 * sub, width)
    recv = lax.all_to_all(send, "ctx", 0, 0, tiled=True)
    recv = recv.reshape(GROUPS, MEMBERS, 2, sub, width)
    return recv.transpose(0, 2, 3, 1, 4).reshape(seqs, 2, block_len, width)


def solution(mesh):
    placed = (
        P("ctx", None, "mp"),
        P(None, "ctx", "mp"),
        P(),
        P(),
        P(),
        P(),
        P(None, "mp"),
        P("mp"),
        P(None, None, "mp"),
        P("mp"),
    )
    return jax.shard_map(
        per_device,
        mesh=mesh,
        in_specs=placed,
        out_specs=P(None, "ctx", None, "mp"),
        check_vma=False,
    )
```

```python
import functools
import math

import jax
import jax.numpy as jnp
from jax import lax
from jax.experimental import pallas as pl
from jax.experimental.pallas import tpu as pltpu
from jax.sharding import PartitionSpec as P

HEAD = 128
NEG_FILL = -1e30
ROPE_BASE = 1000000.0
GROUPS = 4
MEMBERS = 8
DEVICES = GROUPS * MEMBERS
PLANES = 8
MULTIPLY_AT = (1, 2, 3)
STEP = 64
PART = 16
TEXT = 2
SMALL_VMEM = 16 * 1024 * 1024
MID_VMEM = 24 * 1024 * 1024
VMEM_SPEC = pl.BlockSpec(memory_space=pltpu.VMEM)
SMEM_SPEC = pl.BlockSpec(memory_space=pltpu.SMEM)
HBM_SPEC = pl.BlockSpec(memory_space=pltpu.HBM)


def in_hbm(*arrays):
    return [pltpu.with_memory_space_constraint(array, pltpu.HBM) for array in arrays]


def shifted(n, by):
    return [(i, (i + by) % n) for i in range(n)]


def ctx_pairs(move):
    pairs = []
    for i in range(DEVICES):
        y, x, c = move(i // MEMBERS, (i // 2) % 4, i % 2)
        pairs.append((i, (y % 4) * MEMBERS + (x % 4) * 2 + c))
    return pairs


def across(first):
    return ctx_pairs(lambda y, x, c: (y, x ^ (1 if (c == 0) == first else 3), c))


def far_pairs():
    return [
        (i * PLANES + z, i * PLANES + (z + (1 if i % 2 == 0 else -1)) % PLANES)
        for i in range(DEVICES)
        for z in range(PLANES)
    ]


def rope_tables(positions):
    half = HEAD // 2
    frequency = ROPE_BASE ** (-(jnp.arange(half, dtype=jnp.float32) * 2.0) / HEAD)
    angles = positions.astype(jnp.float32)[:, None] * frequency
    cosine, sine = jnp.cos(angles), jnp.sin(angles)
    return jnp.concatenate([cosine, cosine], -1), jnp.concatenate([-sine, sine], -1)


def rows_of(refs):
    return refs[0][...] if len(refs) == 1 else jnp.concatenate([r[...] for r in refs], axis=0)


def products_kernel(groups, halves, fresh, owners_ref, wq_hbm, wk_hbm, *refs):
    wq_ref, wk_ref, sems = refs[-3:]
    q_out, k_out = refs[-5:-3]
    feat = wq_ref.shape[1]
    copies = []
    for i in range(groups):
        at = pl.ds(pl.multiple_of(owners_ref[i] * feat, feat), feat)
        for n, (src, dst) in enumerate(((wq_hbm, wq_ref), (wk_hbm, wk_ref))):
            copy = pltpu.make_async_copy(src.at[at, :], dst.at[i], sems.at[n, i])
            copy.start()
            copies.append(copy)
    q = None if fresh else refs[-7][...]
    k = None if fresh else refs[-6][...]
    for i in range(groups):
        copies[2 * i].wait()
        copies[2 * i + 1].wait()
        rows = rows_of(refs[i * halves : (i + 1) * halves])
        more_q = jnp.dot(rows, wq_ref[i], preferred_element_type=jnp.float32)
        more_k = jnp.dot(rows, wk_ref[i], preferred_element_type=jnp.float32)
        q = more_q if q is None else q + more_q
        k = more_k if k is None else k + more_k
    q_out[...] = q
    k_out[...] = k


def add_products(sums, parts, owners, w_query, kv_flat):
    halves, groups = len(parts[0]), len(parts)
    feat = parts[0][0].shape[1]
    count = sum(part.shape[0] for part in parts[0])
    q_cols, k_cols = w_query.shape[1], kv_flat.shape[1]
    args = sum(parts, []) + list(sums or ())
    return pl.pallas_call(
        functools.partial(products_kernel, groups, halves, sums is None),
        in_specs=[SMEM_SPEC, HBM_SPEC, HBM_SPEC] + [VMEM_SPEC] * len(args),
        out_specs=[VMEM_SPEC] * 2,
        out_shape=[
            jax.ShapeDtypeStruct((count, q_cols), jnp.float32),
            jax.ShapeDtypeStruct((count, k_cols), jnp.float32),
        ],
        scratch_shapes=[
            pltpu.VMEM((groups, feat, q_cols), jnp.bfloat16),
            pltpu.VMEM((groups, feat, k_cols), jnp.bfloat16),
            pltpu.SemaphoreType.DMA((2, groups)),
        ],
        compiler_params=pltpu.CompilerParams(vmem_limit_bytes=SMALL_VMEM),
        cost_estimate=pl.CostEstimate(
            flops=4 * groups * count * feat * (q_cols + k_cols),
            bytes_accessed=groups * feat * (q_cols + k_cols) * 2,
            transcendentals=0,
        ),
    )(jnp.stack(owners).astype(jnp.int32), *in_hbm(w_query, kv_flat), *args)


def rotated(x, cosine, sine):
    return (x * cosine + pltpu.roll(x, HEAD // 2, 1) * sine).astype(jnp.bfloat16)


def finish_kernel(halves, keys, owner_ref, w_hbm, *refs):
    sum_ref, cos_ref, sin_ref, bias_ref, o_ref, w_ref, sem = refs[halves:]
    feat = w_ref.shape[0]
    at = pl.ds(pl.multiple_of(owner_ref[0] * feat, feat), feat)
    copy = pltpu.make_async_copy(w_hbm.at[at, :], w_ref, sem)
    copy.start()
    rows = rows_of(refs[:halves])
    copy.wait()
    out = sum_ref[...] + jnp.dot(rows, w_ref[...], preferred_element_type=jnp.float32)
    bias = bias_ref[...].astype(jnp.float32)
    if keys:
        o_ref[:, :HEAD] = rotated(out[:, :HEAD], cos_ref[...], sin_ref[...])
        o_ref[:, HEAD:] = (out[:, HEAD:] + bias).astype(jnp.bfloat16)
        return
    out = out + bias
    for h in range(out.shape[1] // HEAD):
        at = slice(h * HEAD, (h + 1) * HEAD)
        o_ref[:, at] = rotated(out[:, at], cos_ref[...], sin_ref[...])


def finish(keys, total, far, owner, weight, cosine, sine, bias):
    (count, cols), feat = total.shape, far[0].shape[1]
    args = [*far, total, cosine, sine, bias.reshape(1, -1)]
    return pl.pallas_call(
        functools.partial(finish_kernel, len(far), keys),
        in_specs=[SMEM_SPEC, HBM_SPEC] + [VMEM_SPEC] * len(args),
        out_specs=VMEM_SPEC,
        out_shape=jax.ShapeDtypeStruct((count, cols), jnp.bfloat16),
        scratch_shapes=[pltpu.VMEM((feat, cols), jnp.bfloat16), pltpu.SemaphoreType.DMA],
        compiler_params=pltpu.CompilerParams(vmem_limit_bytes=SMALL_VMEM),
        cost_estimate=pl.CostEstimate(
            flops=4 * count * feat * cols, bytes_accessed=2000000, transcendentals=0
        ),
    )(owner.reshape(1).astype(jnp.int32), *in_hbm(weight), *args)


def one_hot(hit):
    return jnp.where(hit, 1.0, 0.0).astype(jnp.bfloat16)


def iotas(shape):
    return lax.broadcasted_iota(jnp.int32, shape, 0), lax.broadcasted_iota(jnp.int32, shape, 1)


def pack_kernel(clips_here, cand_ref, slot_ref, me_ref, clip_hbm, text_ref, o_ref, held_ref, sem):
    me = me_ref[0]
    which = jnp.int32(0)
    for s in range(cand_ref.shape[0]):
        for k in range(cand_ref.shape[1]):
            slot = slot_ref[cand_ref[s, k]]
            which = jnp.where(slot // clips_here == me, slot % clips_here, which)
    copy = pltpu.make_async_copy(clip_hbm.at[which], held_ref, sem)
    copy.start()
    feat = held_ref.shape[1]
    folds = feat // HEAD
    rows = PART * MEMBERS
    to, at = iotas((rows, PART))
    m, r = to // PART, to % PART
    for y in range(GROUPS):
        text = text_ref[y]
        beside = jnp.zeros((rows, HEAD), jnp.float32)
        for fold in range(folds):
            hit = (r % folds == fold) & (r < TEXT * folds) & (at == m + MEMBERS * (r // folds))
            beside = beside + jnp.dot(
                one_hot(hit), text[:, fold * HEAD : (fold + 1) * HEAD],
                preferred_element_type=jnp.float32,
            )
        o_ref[pl.ds(y * MEMBERS, MEMBERS), :, feat:] = beside.astype(jnp.bfloat16).reshape(
            MEMBERS, PART, HEAD
        )
    to, at = iotas((rows, rows))
    pick = one_hot(at == MEMBERS * (to % PART) + to // PART)
    copy.wait()
    for y in range(GROUPS):
        out = jnp.dot(pick, held_ref[rows * y : rows * (y + 1)], preferred_element_type=jnp.float32)
        o_ref[pl.ds(y * MEMBERS, MEMBERS), :, :feat] = out.astype(jnp.bfloat16).reshape(
            MEMBERS, PART, feat
        )


def pack(candidates, clip_slot, me, clip_store, text_tokens):
    clips_here, clip_len, feat = clip_store.shape
    return pl.pallas_call(
        functools.partial(pack_kernel, clips_here),
        out_shape=jax.ShapeDtypeStruct((DEVICES, PART, feat + HEAD), jnp.bfloat16),
        in_specs=[SMEM_SPEC] * 3 + [HBM_SPEC, VMEM_SPEC],
        out_specs=VMEM_SPEC,
        scratch_shapes=[pltpu.VMEM((clip_len, feat), jnp.bfloat16), pltpu.SemaphoreType.DMA],
        compiler_params=pltpu.CompilerParams(vmem_limit_bytes=SMALL_VMEM),
    )(*in_hbm(candidates, clip_slot), me.reshape(1).astype(jnp.int32), *in_hbm(clip_store, text_tokens))


def unpack_kernel(clips_here, cand_ref, slot_ref, group_ref, sent_ref, own_ref, *out_refs):
    group = group_ref[0]
    feat = own_ref.shape[1]
    folds = feat // HEAD
    beside = sent_ref[:, :, feat:].reshape(DEVICES * PART, HEAD)
    to, at = iotas((TEXT * DEVICES, DEVICES * PART))
    for fold in range(folds):
        hit = at == (to // TEXT) * PART + (to % TEXT) * folds + fold
        own_ref[:STEP, fold * HEAD : (fold + 1) * HEAD] = jnp.dot(
            one_hot(hit), beside, preferred_element_type=jnp.float32
        ).astype(jnp.bfloat16)
    cands = cand_ref.shape[1]
    for dy in range(GROUPS):
        seq = (group + dy) % GROUPS
        for k in range(cands):
            source = slot_ref[cand_ref[seq, k]] // clips_here
            rows = sent_ref[source, :, :feat]
            if dy == 0:
                own_ref[STEP + PART * k : STEP + PART * (k + 1)] = rows
            else:
                out_refs[dy - 1][PART * k : PART * (k + 1)] = rows


def unpack(candidates, clip_slot, group, sent, clips_here):
    feat = sent.shape[2] - HEAD
    shapes = [(2 * STEP, feat)] + [(STEP, feat)] * (GROUPS - 1)
    return pl.pallas_call(
        functools.partial(unpack_kernel, clips_here),
        out_shape=[jax.ShapeDtypeStruct(s, jnp.bfloat16) for s in shapes],
        in_specs=[SMEM_SPEC] * 3 + [VMEM_SPEC],
        out_specs=[VMEM_SPEC] * GROUPS,
        compiler_params=pltpu.CompilerParams(vmem_limit_bytes=SMALL_VMEM),
    )(*in_hbm(candidates, clip_slot), group.reshape(1).astype(jnp.int32), sent)


def attend_kernel(heads, clips, info_ref, q_ref, *refs):
    o_ref, key_refs = refs[-1], refs[:-1]
    group, member = info_ref[0], info_ref[1]
    my_x, my_core = member // 2, member % 2
    scale = math.log2(math.e) / math.sqrt(HEAD)

    def spans(part):
        if part == clips:
            return [(0, STEP)]
        return [(STEP + dy * STEP + PART * part, PART) for dy in range(GROUPS)]

    def idx_of(row, part):
        if part == clips:
            return row
        return ((group + GROUPS - row // PART) % GROUPS) * PART + row % PART

    keys_step = MEMBERS * STEP
    lane = lax.broadcasted_iota(jnp.int32, (STEP, keys_step), 1)
    row = lax.broadcasted_iota(jnp.int32, (STEP, keys_step), 0)
    slot = lane // STEP
    core = (my_core + slot // 4) % 2
    by_near, by_far = jnp.where(core == 0, 1, 3), jnp.where(core == 0, 3, 1)
    x = my_x ^ jnp.where(slot % 2 == 1, by_near, 0) ^ jnp.where((slot // 2) % 2 == 1, by_far, 0)
    k_mem = 2 * x + core

    def gather(part, at):
        return jnp.concatenate(
            [
                ref[piece, pl.ds(first, n), at : at + HEAD]
                for ref in key_refs
                for piece in range(2)
                for first, n in spans(part)
            ],
            axis=0,
        )

    def tiles(array):
        return [array[:, n : n + HEAD] for n in range(0, keys_step, HEAD)]

    for part in range(clips + 1):
        k_pos = MEMBERS * idx_of(lane % STEP, part) + k_mem
        q_pos = MEMBERS * idx_of(row, part) + member
        allowed = jnp.concatenate([k_pos <= q_pos] * heads, axis=0)
        q = jnp.concatenate(
            [
                q_ref[pl.ds(first, n), h * HEAD : (h + 1) * HEAD]
                for h in range(heads)
                for first, n in spans(part)
            ],
            axis=0,
        )
        scores = []
        for kp in range(part + 1):
            s = lax.dot_general(
                q, gather(kp, 0), (((1,), (1,)), ((), ())), preferred_element_type=jnp.float32
            ) * scale
            if kp == part:
                s = jnp.where(allowed, s, NEG_FILL)
            scores.append(s)
        top = functools.reduce(jnp.maximum, [tile for s in scores for tile in tiles(s)])
        top = jnp.max(top, axis=-1, keepdims=True)
        total, acc = None, None
        for kp, s in enumerate(scores):
            w = jnp.exp2(s - top)
            more = functools.reduce(jnp.add, tiles(w))
            total = more if total is None else total + more
            more = jnp.dot(
                w.astype(jnp.bfloat16), gather(kp, HEAD), preferred_element_type=jnp.float32
            )
            acc = more if acc is None else acc + more
        total = jnp.sum(total, axis=-1, keepdims=True)
        out = (acc / total).astype(jnp.bfloat16)
        for h in range(heads):
            at = slice(h * HEAD, (h + 1) * HEAD)
            if part == clips:
                o_ref[pl.ds(part * STEP, STEP), at] = out[h * STEP : (h + 1) * STEP]
                continue
            for dy in range(GROUPS):
                y = (group + GROUPS - dy) % GROUPS
                to = pl.ds(pl.multiple_of(part * STEP + y * PART, PART), PART)
                first = h * STEP + dy * PART
                o_ref[to, at] = out[first : first + PART]


def attend(info, q, pieces, heads, clips):
    return pl.pallas_call(
        functools.partial(attend_kernel, heads, clips),
        out_shape=jax.ShapeDtypeStruct(q.shape, jnp.bfloat16),
        in_specs=[SMEM_SPEC] + [VMEM_SPEC] * (1 + len(pieces)),
        out_specs=VMEM_SPEC,
        compiler_params=pltpu.CompilerParams(vmem_limit_bytes=MID_VMEM),
        cost_estimate=pl.CostEstimate(
            flops=1300000000, bytes_accessed=4000000, transcendentals=2500000
        ),
    )(info, q, *pieces)


def per_device(
    clip_store,
    text_tokens,
    candidates,
    clip_slot,
    text_positions,
    block_order,
    w_query,
    b_query,
    key_value_weight,
    value_offset_bias,
):
    me = lax.axis_index("ctx")
    plane = lax.axis_index("mp")
    group, member = me // MEMBERS, me % MEMBERS
    core = member % 2
    clips_here, clip_len, feat = clip_store.shape
    seqs, cands = candidates.shape
    text_len = text_positions.shape[1]
    width = w_query.shape[1]
    heads = width // HEAD

    sent = pack(candidates, clip_slot, me, clip_store, text_tokens)
    sent = lax.all_to_all(sent, "ctx", 0, 0, tiled=True)

    kv_flat = key_value_weight.reshape(key_value_weight.shape[0], -1)
    text_at = lax.dynamic_index_in_dim(
        lax.dynamic_index_in_dim(text_positions, group, 0, keepdims=False).reshape(-1, MEMBERS),
        member, 1, keepdims=False,
    )
    clip_idx = STEP * jnp.arange(cands)[:, None] + jnp.arange(PART)[None, :]

    def clip_pos(dy):
        y = (group - dy) % GROUPS
        return (MEMBERS * (clip_idx + PART * y) + member).astype(jnp.int32).reshape(-1)

    cosine, sine = rope_tables(jnp.concatenate([text_at] + [clip_pos(dy) for dy in range(GROUPS)]))
    sent, kv_flat, cosine, sine = lax.optimization_barrier((sent, kv_flat, cosine, sine))

    first, *others = unpack(candidates, clip_slot, group, sent, clips_here)
    arrived = [
        lax.ppermute(out, "ctx", ctx_pairs(lambda y, x, c, dy=dy: (y + dy, x, c)))
        for dy, out in enumerate(others, 1)
    ]
    first, arrived[0] = lax.optimization_barrier((first, arrived[0]))
    own = [first, jnp.concatenate(arrived, 0)]

    fwd, bwd = list(own), list(own)
    sums, parts, owners = None, [own], [plane]
    for hop in range(1, PLANES // 2):
        for h in range(len(own)):
            fwd[h] = lax.ppermute(fwd[h], "mp", shifted(PLANES, 1))
            bwd[h] = lax.ppermute(bwd[h], "mp", shifted(PLANES, -1))
        if hop in MULTIPLY_AT:
            sums = add_products(sums, parts, owners, w_query, kv_flat)
            fwd[-1], bwd[-1], sums = lax.optimization_barrier((fwd[-1], bwd[-1], sums))
            parts, owners = [], []
        parts += [list(fwd), list(bwd)]
        owners += [(plane - hop) % PLANES, (plane + hop) % PLANES]
    far = [
        lax.ppermute(jnp.where(core == 0, fwd[h], bwd[h]), ("ctx", "mp"), far_pairs())
        for h in range(len(own))
    ]
    sums = add_products(sums, parts, owners, w_query, kv_flat)
    far[-1], sums = lax.optimization_barrier((far[-1], sums))
    opposite = (plane + PLANES // 2) % PLANES
    kv = finish(True, sums[1], far, opposite, kv_flat, cosine, sine, value_offset_bias)
    q = finish(False, sums[0], far, opposite, w_query, cosine, sine, b_query)

    beside = lax.ppermute(kv, "ctx", across(True))
    beside, q = lax.optimization_barrier((beside, q))
    near = jnp.stack([kv, beside])
    off = lax.ppermute(near, "ctx", across(False))
    swap = ctx_pairs(lambda y, x, c: (y, x, 1 - c))
    pieces = [near, off, lax.ppermute(near, "ctx", swap), lax.ppermute(off, "ctx", swap)]

    info = jnp.stack([group, member]).astype(jnp.int32)
    out = attend(info, q, pieces, heads, cands)

    blocks = block_order.shape[0]
    block_len = (cands * clip_len + text_len) // blocks
    sub = block_len // MEMBERS
    send = jnp.take(out.reshape(blocks, sub, width), block_order, axis=0)
    send = send.reshape(DEVICES, 2 * sub, width)
    recv = lax.all_to_all(send, "ctx", 0, 0, tiled=True)
    recv = recv.reshape(GROUPS, MEMBERS, 2, sub, width)
    return recv.transpose(0, 2, 3, 1, 4).reshape(seqs, 2, block_len, width)


def solution(mesh):
    placed = (
        P("ctx", None, "mp"),
        P(None, "ctx", "mp"),
        P(),
        P(),
        P(),
        P(),
        P(None, "mp"),
        P("mp"),
        P(None, None, "mp"),
        P("mp"),
    )
    return jax.shard_map(
        per_device,
        mesh=mesh,
        in_specs=placed,
        out_specs=P(None, "ctx", None, "mp"),
        check_vma=False,
    )
```

```python
import functools
import math

import jax
import jax.numpy as jnp
from jax import lax
from jax.experimental import pallas as pl
from jax.experimental.pallas import tpu as pltpu
from jax.sharding import PartitionSpec as P

HEAD = 128
NEG_FILL = -1e30
ROPE_BASE = 1000000.0
GROUPS = 4
MEMBERS = 8
DEVICES = GROUPS * MEMBERS
PLANES = 8
MULTIPLY_AT = (1, 2, 3)
STEP = 64
PART = 16
TEXT = 2
SMALL_VMEM = 16 * 1024 * 1024
MID_VMEM = 24 * 1024 * 1024
VMEM_SPEC = pl.BlockSpec(memory_space=pltpu.VMEM)
SMEM_SPEC = pl.BlockSpec(memory_space=pltpu.SMEM)
HBM_SPEC = pl.BlockSpec(memory_space=pltpu.HBM)


def in_hbm(*arrays):
    return [pltpu.with_memory_space_constraint(array, pltpu.HBM) for array in arrays]


def shifted(n, by):
    return [(i, (i + by) % n) for i in range(n)]


def ctx_pairs(move):
    pairs = []
    for i in range(DEVICES):
        y, x, c = move(i // MEMBERS, (i // 2) % 4, i % 2)
        pairs.append((i, (y % 4) * MEMBERS + (x % 4) * 2 + c))
    return pairs


def across(first):
    return ctx_pairs(lambda y, x, c: (y, x ^ (1 if (c == 0) == first else 3), c))


def far_pairs():
    return [
        (i * PLANES + z, i * PLANES + (z + (1 if i % 2 == 0 else -1)) % PLANES)
        for i in range(DEVICES)
        for z in range(PLANES)
    ]


def rope_tables(positions):
    half = HEAD // 2
    frequency = ROPE_BASE ** (-(jnp.arange(half, dtype=jnp.float32) * 2.0) / HEAD)
    angles = positions.astype(jnp.float32)[:, None] * frequency
    cosine, sine = jnp.cos(angles), jnp.sin(angles)
    return jnp.concatenate([cosine, cosine], -1), jnp.concatenate([-sine, sine], -1)


def rows_of(refs):
    return refs[0][...] if len(refs) == 1 else jnp.concatenate([r[...] for r in refs], axis=0)


def products_kernel(groups, halves, fresh, owners_ref, wq_hbm, wk_hbm, *refs):
    wq_ref, wk_ref, sems = refs[-3:]
    q_out, k_out = refs[-5:-3]
    feat = wq_ref.shape[1]
    copies = []
    for i in range(groups):
        at = pl.ds(pl.multiple_of(owners_ref[i] * feat, feat), feat)
        for n, (src, dst) in enumerate(((wq_hbm, wq_ref), (wk_hbm, wk_ref))):
            copy = pltpu.make_async_copy(src.at[at, :], dst.at[i], sems.at[n, i])
            copy.start()
            copies.append(copy)
    q = None if fresh else refs[-7][...]
    k = None if fresh else refs[-6][...]
    for i in range(groups):
        copies[2 * i].wait()
        copies[2 * i + 1].wait()
        rows = rows_of(refs[i * halves : (i + 1) * halves])
        more_q = jnp.dot(rows, wq_ref[i], preferred_element_type=jnp.float32)
        more_k = jnp.dot(rows, wk_ref[i], preferred_element_type=jnp.float32)
        q = more_q if q is None else q + more_q
        k = more_k if k is None else k + more_k
    q_out[...] = q
    k_out[...] = k


def add_products(sums, parts, owners, w_query, kv_flat):
    halves, groups = len(parts[0]), len(parts)
    feat = parts[0][0].shape[1]
    count = sum(part.shape[0] for part in parts[0])
    q_cols, k_cols = w_query.shape[1], kv_flat.shape[1]
    args = sum(parts, []) + list(sums or ())
    return pl.pallas_call(
        functools.partial(products_kernel, groups, halves, sums is None),
        in_specs=[SMEM_SPEC, HBM_SPEC, HBM_SPEC] + [VMEM_SPEC] * len(args),
        out_specs=[VMEM_SPEC] * 2,
        out_shape=[
            jax.ShapeDtypeStruct((count, q_cols), jnp.float32),
            jax.ShapeDtypeStruct((count, k_cols), jnp.float32),
        ],
        scratch_shapes=[
            pltpu.VMEM((groups, feat, q_cols), jnp.bfloat16),
            pltpu.VMEM((groups, feat, k_cols), jnp.bfloat16),
            pltpu.SemaphoreType.DMA((2, groups)),
        ],
        compiler_params=pltpu.CompilerParams(vmem_limit_bytes=SMALL_VMEM),
        cost_estimate=pl.CostEstimate(
            flops=4 * groups * count * feat * (q_cols + k_cols),
            bytes_accessed=groups * feat * (q_cols + k_cols) * 2,
            transcendentals=0,
        ),
    )(jnp.stack(owners).astype(jnp.int32), *in_hbm(w_query, kv_flat), *args)


def rotated(x, cosine, sine):
    return (x * cosine + pltpu.roll(x, HEAD // 2, 1) * sine).astype(jnp.bfloat16)


def finish_kernel(halves, keys, owner_ref, w_hbm, *refs):
    sum_ref, cos_ref, sin_ref, bias_ref, o_ref, w_ref, sem = refs[halves:]
    feat = w_ref.shape[0]
    at = pl.ds(pl.multiple_of(owner_ref[0] * feat, feat), feat)
    copy = pltpu.make_async_copy(w_hbm.at[at, :], w_ref, sem)
    copy.start()
    rows = rows_of(refs[:halves])
    copy.wait()
    out = sum_ref[...] + jnp.dot(rows, w_ref[...], preferred_element_type=jnp.float32)
    bias = bias_ref[...].astype(jnp.float32)
    if keys:
        o_ref[:, :HEAD] = rotated(out[:, :HEAD], cos_ref[...], sin_ref[...])
        o_ref[:, HEAD:] = (out[:, HEAD:] + bias).astype(jnp.bfloat16)
        return
    out = out + bias
    for h in range(out.shape[1] // HEAD):
        at = slice(h * HEAD, (h + 1) * HEAD)
        o_ref[:, at] = rotated(out[:, at], cos_ref[...], sin_ref[...])


def finish(keys, total, far, owner, weight, cosine, sine, bias):
    (count, cols), feat = total.shape, far[0].shape[1]
    args = [*far, total, cosine, sine, bias.reshape(1, -1)]
    return pl.pallas_call(
        functools.partial(finish_kernel, len(far), keys),
        in_specs=[SMEM_SPEC, HBM_SPEC] + [VMEM_SPEC] * len(args),
        out_specs=VMEM_SPEC,
        out_shape=jax.ShapeDtypeStruct((count, cols), jnp.bfloat16),
        scratch_shapes=[pltpu.VMEM((feat, cols), jnp.bfloat16), pltpu.SemaphoreType.DMA],
        compiler_params=pltpu.CompilerParams(vmem_limit_bytes=SMALL_VMEM),
        cost_estimate=pl.CostEstimate(
            flops=4 * count * feat * cols, bytes_accessed=2000000, transcendentals=0
        ),
    )(owner.reshape(1).astype(jnp.int32), *in_hbm(weight), *args)


def one_hot(hit):
    return jnp.where(hit, 1.0, 0.0).astype(jnp.bfloat16)


def iotas(shape):
    return lax.broadcasted_iota(jnp.int32, shape, 0), lax.broadcasted_iota(jnp.int32, shape, 1)


def pack_kernel(clips_here, cand_ref, slot_ref, me_ref, clip_hbm, text_ref, o_ref, held_ref, sem):
    me = me_ref[0]
    which = jnp.int32(0)
    for s in range(cand_ref.shape[0]):
        for k in range(cand_ref.shape[1]):
            slot = slot_ref[cand_ref[s, k]]
            which = jnp.where(slot // clips_here == me, slot % clips_here, which)
    copy = pltpu.make_async_copy(clip_hbm.at[which], held_ref, sem)
    copy.start()
    feat = held_ref.shape[1]
    folds = feat // HEAD
    rows = PART * MEMBERS
    to, at = iotas((rows, PART))
    m, r = to // PART, to % PART
    for y in range(GROUPS):
        text = text_ref[y]
        beside = jnp.zeros((rows, HEAD), jnp.float32)
        for fold in range(folds):
            hit = (r % folds == fold) & (r < TEXT * folds) & (at == m + MEMBERS * (r // folds))
            beside = beside + jnp.dot(
                one_hot(hit), text[:, fold * HEAD : (fold + 1) * HEAD],
                preferred_element_type=jnp.float32,
            )
        o_ref[pl.ds(y * MEMBERS, MEMBERS), :, feat:] = beside.astype(jnp.bfloat16).reshape(
            MEMBERS, PART, HEAD
        )
    to, at = iotas((rows, rows))
    pick = one_hot(at == MEMBERS * (to % PART) + to // PART)
    copy.wait()
    for y in range(GROUPS):
        out = jnp.dot(pick, held_ref[rows * y : rows * (y + 1)], preferred_element_type=jnp.float32)
        o_ref[pl.ds(y * MEMBERS, MEMBERS), :, :feat] = out.astype(jnp.bfloat16).reshape(
            MEMBERS, PART, feat
        )


def pack(candidates, clip_slot, me, clip_store, text_tokens):
    clips_here, clip_len, feat = clip_store.shape
    return pl.pallas_call(
        functools.partial(pack_kernel, clips_here),
        out_shape=jax.ShapeDtypeStruct((DEVICES, PART, feat + HEAD), jnp.bfloat16),
        in_specs=[SMEM_SPEC] * 3 + [HBM_SPEC, VMEM_SPEC],
        out_specs=VMEM_SPEC,
        scratch_shapes=[pltpu.VMEM((clip_len, feat), jnp.bfloat16), pltpu.SemaphoreType.DMA],
        compiler_params=pltpu.CompilerParams(vmem_limit_bytes=SMALL_VMEM),
    )(*in_hbm(candidates, clip_slot), me.reshape(1).astype(jnp.int32), *in_hbm(clip_store, text_tokens))


def unpack_kernel(clips_here, cand_ref, slot_ref, group_ref, sent_ref, own_ref, *out_refs):
    group = group_ref[0]
    feat = own_ref.shape[1]
    folds = feat // HEAD
    beside = sent_ref[:, :, feat:].reshape(DEVICES * PART, HEAD)
    to, at = iotas((TEXT * DEVICES, DEVICES * PART))
    for fold in range(folds):
        hit = at == (to // TEXT) * PART + (to % TEXT) * folds + fold
        own_ref[:STEP, fold * HEAD : (fold + 1) * HEAD] = jnp.dot(
            one_hot(hit), beside, preferred_element_type=jnp.float32
        ).astype(jnp.bfloat16)
    cands = cand_ref.shape[1]
    for dy in range(GROUPS):
        seq = (group + dy) % GROUPS
        for k in range(cands):
            source = slot_ref[cand_ref[seq, k]] // clips_here
            rows = sent_ref[source, :, :feat]
            if dy == 0:
                own_ref[STEP + PART * k : STEP + PART * (k + 1)] = rows
            else:
                out_refs[dy - 1][PART * k : PART * (k + 1)] = rows


def unpack(candidates, clip_slot, group, sent, clips_here):
    feat = sent.shape[2] - HEAD
    shapes = [(2 * STEP, feat)] + [(STEP, feat)] * (GROUPS - 1)
    return pl.pallas_call(
        functools.partial(unpack_kernel, clips_here),
        out_shape=[jax.ShapeDtypeStruct(s, jnp.bfloat16) for s in shapes],
        in_specs=[SMEM_SPEC] * 3 + [VMEM_SPEC],
        out_specs=[VMEM_SPEC] * GROUPS,
        compiler_params=pltpu.CompilerParams(vmem_limit_bytes=SMALL_VMEM),
    )(*in_hbm(candidates, clip_slot), group.reshape(1).astype(jnp.int32), sent)


def attend_kernel(heads, clips, info_ref, q_ref, to_ref, *refs):
    o_ref, out_ref, key_refs = refs[-2], refs[-1], refs[:-2]
    group, member = info_ref[0], info_ref[1]
    my_x, my_core = member // 2, member % 2
    scale = math.log2(math.e) / math.sqrt(HEAD)

    def spans(part):
        if part == clips:
            return [(0, STEP)]
        return [(STEP + dy * STEP + PART * part, PART) for dy in range(GROUPS)]

    def idx_of(row, part):
        if part == clips:
            return row
        return ((group + GROUPS - row // PART) % GROUPS) * PART + row % PART

    keys_step = MEMBERS * STEP
    lane = lax.broadcasted_iota(jnp.int32, (STEP, keys_step), 1)
    row = lax.broadcasted_iota(jnp.int32, (STEP, keys_step), 0)
    slot = lane // STEP
    core = (my_core + slot // 4) % 2
    by_near, by_far = jnp.where(core == 0, 1, 3), jnp.where(core == 0, 3, 1)
    x = my_x ^ jnp.where(slot % 2 == 1, by_near, 0) ^ jnp.where((slot // 2) % 2 == 1, by_far, 0)
    k_mem = 2 * x + core

    def gather(part, at):
        return jnp.concatenate(
            [
                ref[piece, pl.ds(first, n), at : at + HEAD]
                for ref in key_refs
                for piece in range(2)
                for first, n in spans(part)
            ],
            axis=0,
        )

    def tiles(array):
        return [array[:, n : n + HEAD] for n in range(0, keys_step, HEAD)]

    for part in range(clips + 1):
        k_pos = MEMBERS * idx_of(lane % STEP, part) + k_mem
        q_pos = MEMBERS * idx_of(row, part) + member
        allowed = jnp.concatenate([k_pos <= q_pos] * heads, axis=0)
        q = jnp.concatenate(
            [
                q_ref[pl.ds(first, n), h * HEAD : (h + 1) * HEAD]
                for h in range(heads)
                for first, n in spans(part)
            ],
            axis=0,
        )
        scores = []
        for kp in range(part + 1):
            s = lax.dot_general(
                q, gather(kp, 0), (((1,), (1,)), ((), ())), preferred_element_type=jnp.float32
            ) * scale
            if kp == part:
                s = jnp.where(allowed, s, NEG_FILL)
            scores.append(s)
        top = functools.reduce(jnp.maximum, [tile for s in scores for tile in tiles(s)])
        top = jnp.max(top, axis=-1, keepdims=True)
        total, acc = None, None
        for kp, s in enumerate(scores):
            w = jnp.exp2(s - top)
            more = functools.reduce(jnp.add, tiles(w))
            total = more if total is None else total + more
            more = jnp.dot(
                w.astype(jnp.bfloat16), gather(kp, HEAD), preferred_element_type=jnp.float32
            )
            acc = more if acc is None else acc + more
        total = jnp.sum(total, axis=-1, keepdims=True)
        out = (acc / total).astype(jnp.bfloat16)
        for h in range(heads):
            at = slice(h * HEAD, (h + 1) * HEAD)
            if part == clips:
                out_ref[pl.ds(part * STEP, STEP), at] = out[h * STEP : (h + 1) * STEP]
                continue
            for dy in range(GROUPS):
                y = (group + GROUPS - dy) % GROUPS
                to = pl.ds(pl.multiple_of(part * STEP + y * PART, PART), PART)
                first = h * STEP + dy * PART
                out_ref[to, at] = out[first : first + PART]
    _, at = iotas((o_ref.shape[0], out_ref.shape[0]))
    pick = one_hot(at == to_ref[...])
    o_ref[...] = jnp.dot(pick, out_ref[...], preferred_element_type=jnp.float32).astype(
        jnp.bfloat16
    )


def attend(info, q, to, pieces, heads, clips):
    return pl.pallas_call(
        functools.partial(attend_kernel, heads, clips),
        out_shape=jax.ShapeDtypeStruct(q.shape, jnp.bfloat16),
        in_specs=[SMEM_SPEC] + [VMEM_SPEC] * (2 + len(pieces)),
        out_specs=VMEM_SPEC,
        scratch_shapes=[pltpu.VMEM(q.shape, jnp.bfloat16)],
        compiler_params=pltpu.CompilerParams(vmem_limit_bytes=MID_VMEM),
        cost_estimate=pl.CostEstimate(
            flops=1300000000, bytes_accessed=4000000, transcendentals=2500000
        ),
    )(info, q, to, *pieces)


def per_device(
    clip_store,
    text_tokens,
    candidates,
    clip_slot,
    text_positions,
    block_order,
    w_query,
    b_query,
    key_value_weight,
    value_offset_bias,
):
    me = lax.axis_index("ctx")
    plane = lax.axis_index("mp")
    group, member = me // MEMBERS, me % MEMBERS
    core = member % 2
    clips_here, clip_len, feat = clip_store.shape
    seqs, cands = candidates.shape
    text_len = text_positions.shape[1]
    width = w_query.shape[1]
    heads = width // HEAD

    sent = pack(candidates, clip_slot, me, clip_store, text_tokens)
    sent = lax.all_to_all(sent, "ctx", 0, 0, tiled=True)

    kv_flat = key_value_weight.reshape(key_value_weight.shape[0], -1)
    text_at = lax.dynamic_index_in_dim(
        lax.dynamic_index_in_dim(text_positions, group, 0, keepdims=False).reshape(-1, MEMBERS),
        member, 1, keepdims=False,
    )
    clip_idx = STEP * jnp.arange(cands)[:, None] + jnp.arange(PART)[None, :]

    def clip_pos(dy):
        y = (group - dy) % GROUPS
        return (MEMBERS * (clip_idx + PART * y) + member).astype(jnp.int32).reshape(-1)

    cosine, sine = rope_tables(jnp.concatenate([text_at] + [clip_pos(dy) for dy in range(GROUPS)]))
    blocks = block_order.shape[0]
    block_len = (cands * clip_len + text_len) // blocks
    sub = block_len // MEMBERS
    send_from = sub * block_order.reshape(DEVICES, 1, 2) + jnp.arange(sub).reshape(1, sub, 1)
    send_from = send_from.astype(jnp.int32).reshape(-1, 1)
    sent, kv_flat, cosine, sine, send_from = lax.optimization_barrier(
        (sent, kv_flat, cosine, sine, send_from)
    )

    first, *others = unpack(candidates, clip_slot, group, sent, clips_here)
    arrived = [
        lax.ppermute(out, "ctx", ctx_pairs(lambda y, x, c, dy=dy: (y + dy, x, c)))
        for dy, out in enumerate(others, 1)
    ]
    first, arrived[0] = lax.optimization_barrier((first, arrived[0]))
    own = [first, jnp.concatenate(arrived, 0)]

    fwd, bwd = list(own), list(own)
    sums, parts, owners = None, [own], [plane]
    for hop in range(1, PLANES // 2):
        for h in range(len(own)):
            fwd[h] = lax.ppermute(fwd[h], "mp", shifted(PLANES, 1))
            bwd[h] = lax.ppermute(bwd[h], "mp", shifted(PLANES, -1))
        if hop in MULTIPLY_AT:
            sums = add_products(sums, parts, owners, w_query, kv_flat)
            fwd[-1], bwd[-1], sums = lax.optimization_barrier((fwd[-1], bwd[-1], sums))
            parts, owners = [], []
        parts += [list(fwd), list(bwd)]
        owners += [(plane - hop) % PLANES, (plane + hop) % PLANES]
    far = [
        lax.ppermute(jnp.where(core == 0, fwd[h], bwd[h]), ("ctx", "mp"), far_pairs())
        for h in range(len(own))
    ]
    sums = add_products(sums, parts, owners, w_query, kv_flat)
    far[-1], sums = lax.optimization_barrier((far[-1], sums))
    opposite = (plane + PLANES // 2) % PLANES
    kv = finish(True, sums[1], far, opposite, kv_flat, cosine, sine, value_offset_bias)
    q = finish(False, sums[0], far, opposite, w_query, cosine, sine, b_query)

    beside = lax.ppermute(kv, "ctx", across(True))
    beside, q = lax.optimization_barrier((beside, q))
    near = jnp.stack([kv, beside])
    off = lax.ppermute(near, "ctx", across(False))
    swap = ctx_pairs(lambda y, x, c: (y, x, 1 - c))
    pieces = [near, off, lax.ppermute(near, "ctx", swap), lax.ppermute(off, "ctx", swap)]

    info = jnp.stack([group, member]).astype(jnp.int32)
    out = attend(info, q, send_from, pieces, heads, cands)

    send = out.reshape(DEVICES, sub, 2, width)
    recv = lax.all_to_all(send, "ctx", 0, 0, tiled=True)
    recv = recv.reshape(GROUPS, MEMBERS, sub, 2, width)
    return recv.transpose(0, 3, 2, 1, 4).reshape(seqs, 2, block_len, width)


def solution(mesh):
    placed = (
        P("ctx", None, "mp"),
        P(None, "ctx", "mp"),
        P(),
        P(),
        P(),
        P(),
        P(None, "mp"),
        P("mp"),
        P(None, None, "mp"),
        P("mp"),
    )
    return jax.shard_map(
        per_device,
        mesh=mesh,
        in_specs=placed,
        out_specs=P(None, "ctx", None, "mp"),
        check_vma=False,
    )
```

```python
import functools
import math

import jax
import jax.numpy as jnp
from jax import lax
from jax.experimental import pallas as pl
from jax.experimental.pallas import tpu as pltpu
from jax.sharding import PartitionSpec as P

HEAD = 128
NEG_FILL = -1e30
ROPE_BASE = 1000000.0
GROUPS = 4
MEMBERS = 8
DEVICES = GROUPS * MEMBERS
PLANES = 8
MULTIPLY_AT = (1, 2, 3)
STEP = 64
PART = 16
TEXT = 2
SMALL_VMEM = 16 * 1024 * 1024
MID_VMEM = 24 * 1024 * 1024
VMEM_SPEC = pl.BlockSpec(memory_space=pltpu.VMEM)
SMEM_SPEC = pl.BlockSpec(memory_space=pltpu.SMEM)
HBM_SPEC = pl.BlockSpec(memory_space=pltpu.HBM)


def in_hbm(*arrays):
    return [pltpu.with_memory_space_constraint(array, pltpu.HBM) for array in arrays]


def shifted(n, by):
    return [(i, (i + by) % n) for i in range(n)]


def ctx_pairs(move):
    pairs = []
    for i in range(DEVICES):
        y, x, c = move(i // MEMBERS, (i // 2) % 4, i % 2)
        pairs.append((i, (y % 4) * MEMBERS + (x % 4) * 2 + c))
    return pairs


def far_pairs():
    return [
        (i * PLANES + z, i * PLANES + (z + (1 if i % 2 == 0 else -1)) % PLANES)
        for i in range(DEVICES)
        for z in range(PLANES)
    ]


def rope_tables(positions):
    half = HEAD // 2
    frequency = ROPE_BASE ** (-(jnp.arange(half, dtype=jnp.float32) * 2.0) / HEAD)
    angles = positions.astype(jnp.float32)[:, None] * frequency
    cosine, sine = jnp.cos(angles), jnp.sin(angles)
    return jnp.concatenate([cosine, cosine], -1), jnp.concatenate([-sine, sine], -1)


def rows_of(refs):
    return refs[0][...] if len(refs) == 1 else jnp.concatenate([r[...] for r in refs], axis=0)


def products_kernel(groups, halves, fresh, owners_ref, wq_hbm, wk_hbm, *refs):
    wq_ref, wk_ref, sems = refs[-3:]
    q_out, k_out = refs[-5:-3]
    feat = wq_ref.shape[1]
    copies = []
    for i in range(groups):
        at = pl.ds(pl.multiple_of(owners_ref[i] * feat, feat), feat)
        for n, (src, dst) in enumerate(((wq_hbm, wq_ref), (wk_hbm, wk_ref))):
            copy = pltpu.make_async_copy(src.at[at, :], dst.at[i], sems.at[n, i])
            copy.start()
            copies.append(copy)
    q = None if fresh else refs[-7][...]
    k = None if fresh else refs[-6][...]
    for i in range(groups):
        copies[2 * i].wait()
        copies[2 * i + 1].wait()
        rows = rows_of(refs[i * halves : (i + 1) * halves])
        more_q = jnp.dot(rows, wq_ref[i], preferred_element_type=jnp.float32)
        more_k = jnp.dot(rows, wk_ref[i], preferred_element_type=jnp.float32)
        q = more_q if q is None else q + more_q
        k = more_k if k is None else k + more_k
    q_out[...] = q
    k_out[...] = k


def add_products(sums, parts, owners, w_query, kv_flat):
    halves, groups = len(parts[0]), len(parts)
    feat = parts[0][0].shape[1]
    count = sum(part.shape[0] for part in parts[0])
    q_cols, k_cols = w_query.shape[1], kv_flat.shape[1]
    args = sum(parts, []) + list(sums or ())
    return pl.pallas_call(
        functools.partial(products_kernel, groups, halves, sums is None),
        in_specs=[SMEM_SPEC, HBM_SPEC, HBM_SPEC] + [VMEM_SPEC] * len(args),
        out_specs=[VMEM_SPEC] * 2,
        out_shape=[
            jax.ShapeDtypeStruct((count, q_cols), jnp.float32),
            jax.ShapeDtypeStruct((count, k_cols), jnp.float32),
        ],
        scratch_shapes=[
            pltpu.VMEM((groups, feat, q_cols), jnp.bfloat16),
            pltpu.VMEM((groups, feat, k_cols), jnp.bfloat16),
            pltpu.SemaphoreType.DMA((2, groups)),
        ],
        compiler_params=pltpu.CompilerParams(vmem_limit_bytes=SMALL_VMEM),
        cost_estimate=pl.CostEstimate(
            flops=4 * groups * count * feat * (q_cols + k_cols),
            bytes_accessed=groups * feat * (q_cols + k_cols) * 2,
            transcendentals=0,
        ),
    )(jnp.stack(owners).astype(jnp.int32), *in_hbm(w_query, kv_flat), *args)


def rotated(x, cosine, sine):
    return (x * cosine + pltpu.roll(x, HEAD // 2, 1) * sine).astype(jnp.bfloat16)


def finish_kernel(halves, keys, owner_ref, w_hbm, *refs):
    sum_ref, cos_ref, sin_ref, bias_ref, o_ref, w_ref, sem = refs[halves:]
    feat = w_ref.shape[0]
    at = pl.ds(pl.multiple_of(owner_ref[0] * feat, feat), feat)
    copy = pltpu.make_async_copy(w_hbm.at[at, :], w_ref, sem)
    copy.start()
    rows = rows_of(refs[:halves])
    copy.wait()
    out = sum_ref[...] + jnp.dot(rows, w_ref[...], preferred_element_type=jnp.float32)
    bias = bias_ref[...].astype(jnp.float32)
    if keys:
        o_ref[:, :HEAD] = rotated(out[:, :HEAD], cos_ref[...], sin_ref[...])
        o_ref[:, HEAD:] = (out[:, HEAD:] + bias).astype(jnp.bfloat16)
        return
    out = out + bias
    for h in range(out.shape[1] // HEAD):
        at = slice(h * HEAD, (h + 1) * HEAD)
        o_ref[:, at] = rotated(out[:, at], cos_ref[...], sin_ref[...])


def finish(keys, total, far, owner, weight, cosine, sine, bias):
    (count, cols), feat = total.shape, far[0].shape[1]
    args = [*far, total, cosine, sine, bias.reshape(1, -1)]
    return pl.pallas_call(
        functools.partial(finish_kernel, len(far), keys),
        in_specs=[SMEM_SPEC, HBM_SPEC] + [VMEM_SPEC] * len(args),
        out_specs=VMEM_SPEC,
        out_shape=jax.ShapeDtypeStruct((count, cols), jnp.bfloat16),
        scratch_shapes=[pltpu.VMEM((feat, cols), jnp.bfloat16), pltpu.SemaphoreType.DMA],
        compiler_params=pltpu.CompilerParams(vmem_limit_bytes=SMALL_VMEM),
        cost_estimate=pl.CostEstimate(
            flops=4 * count * feat * cols, bytes_accessed=2000000, transcendentals=0
        ),
    )(owner.reshape(1).astype(jnp.int32), *in_hbm(weight), *args)


def one_hot(hit):
    return jnp.where(hit, 1.0, 0.0).astype(jnp.bfloat16)


def iotas(shape):
    return lax.broadcasted_iota(jnp.int32, shape, 0), lax.broadcasted_iota(jnp.int32, shape, 1)


def pack_kernel(clips_here, cand_ref, slot_ref, me_ref, clip_hbm, text_ref, o_ref, held_ref, sem):
    me = me_ref[0]
    which = jnp.int32(0)
    for s in range(cand_ref.shape[0]):
        for k in range(cand_ref.shape[1]):
            slot = slot_ref[cand_ref[s, k]]
            which = jnp.where(slot // clips_here == me, slot % clips_here, which)
    copy = pltpu.make_async_copy(clip_hbm.at[which], held_ref, sem)
    copy.start()
    feat = held_ref.shape[1]
    folds = feat // HEAD
    rows = PART * MEMBERS
    to, at = iotas((rows, PART))
    m, r = to // PART, to % PART
    for y in range(GROUPS):
        text = text_ref[y]
        beside = jnp.zeros((rows, HEAD), jnp.float32)
        for fold in range(folds):
            hit = (r % folds == fold) & (r < TEXT * folds) & (at == m + MEMBERS * (r // folds))
            beside = beside + jnp.dot(
                one_hot(hit), text[:, fold * HEAD : (fold + 1) * HEAD],
                preferred_element_type=jnp.float32,
            )
        o_ref[pl.ds(y * MEMBERS, MEMBERS), :, feat:] = beside.astype(jnp.bfloat16).reshape(
            MEMBERS, PART, HEAD
        )
    to, at = iotas((rows, rows))
    pick = one_hot(at == MEMBERS * (to % PART) + to // PART)
    copy.wait()
    for y in range(GROUPS):
        out = jnp.dot(pick, held_ref[rows * y : rows * (y + 1)], preferred_element_type=jnp.float32)
        o_ref[pl.ds(y * MEMBERS, MEMBERS), :, :feat] = out.astype(jnp.bfloat16).reshape(
            MEMBERS, PART, feat
        )


def pack(candidates, clip_slot, me, clip_store, text_tokens):
    clips_here, clip_len, feat = clip_store.shape
    return pl.pallas_call(
        functools.partial(pack_kernel, clips_here),
        out_shape=jax.ShapeDtypeStruct((DEVICES, PART, feat + HEAD), jnp.bfloat16),
        in_specs=[SMEM_SPEC] * 3 + [HBM_SPEC, VMEM_SPEC],
        out_specs=VMEM_SPEC,
        scratch_shapes=[pltpu.VMEM((clip_len, feat), jnp.bfloat16), pltpu.SemaphoreType.DMA],
        compiler_params=pltpu.CompilerParams(vmem_limit_bytes=SMALL_VMEM),
    )(*in_hbm(candidates, clip_slot), me.reshape(1).astype(jnp.int32), *in_hbm(clip_store, text_tokens))


def unpack_kernel(clips_here, cand_ref, slot_ref, group_ref, sent_ref, own_ref, *out_refs):
    group = group_ref[0]
    feat = own_ref.shape[1]
    folds = feat // HEAD
    beside = sent_ref[:, :, feat:].reshape(DEVICES * PART, HEAD)
    to, at = iotas((TEXT * DEVICES, DEVICES * PART))
    for fold in range(folds):
        hit = at == (to // TEXT) * PART + (to % TEXT) * folds + fold
        own_ref[:STEP, fold * HEAD : (fold + 1) * HEAD] = jnp.dot(
            one_hot(hit), beside, preferred_element_type=jnp.float32
        ).astype(jnp.bfloat16)
    cands = cand_ref.shape[1]
    for dy in range(GROUPS):
        seq = (group + dy) % GROUPS
        for k in range(cands):
            source = slot_ref[cand_ref[seq, k]] // clips_here
            rows = sent_ref[source, :, :feat]
            if dy == 0:
                own_ref[STEP + PART * k : STEP + PART * (k + 1)] = rows
            else:
                out_refs[dy - 1][PART * k : PART * (k + 1)] = rows


def unpack(candidates, clip_slot, group, sent, clips_here):
    feat = sent.shape[2] - HEAD
    shapes = [(2 * STEP, feat)] + [(STEP, feat)] * (GROUPS - 1)
    return pl.pallas_call(
        functools.partial(unpack_kernel, clips_here),
        out_shape=[jax.ShapeDtypeStruct(s, jnp.bfloat16) for s in shapes],
        in_specs=[SMEM_SPEC] * 3 + [VMEM_SPEC],
        out_specs=[VMEM_SPEC] * GROUPS,
        compiler_params=pltpu.CompilerParams(vmem_limit_bytes=SMALL_VMEM),
    )(*in_hbm(candidates, clip_slot), group.reshape(1).astype(jnp.int32), sent)


def attend_kernel(heads, clips, info_ref, q_ref, to_ref, *refs):
    o_ref, out_ref, key_refs = refs[-2], refs[-1], refs[:-2]
    group, member = info_ref[0], info_ref[1]
    my_x, my_core = member // 2, member % 2
    scale = math.log2(math.e) / math.sqrt(HEAD)

    def spans(part):
        if part == clips:
            return [(0, STEP)]
        return [(STEP + dy * STEP + PART * part, PART) for dy in range(GROUPS)]

    def idx_of(row, part):
        if part == clips:
            return row
        return ((group + GROUPS - row // PART) % GROUPS) * PART + row % PART

    keys_step = MEMBERS * STEP
    lane = lax.broadcasted_iota(jnp.int32, (STEP, keys_step), 1)
    row = lax.broadcasted_iota(jnp.int32, (STEP, keys_step), 0)
    slot = lane // STEP
    pair = slot // 2
    off = jnp.where(pair == 0, 0, jnp.where(pair == 1, 3, pair - 1))
    k_mem = 2 * ((my_x + off) % 4) + (my_core + slot) % 2

    def gather(part, at):
        return jnp.concatenate(
            [
                ref[pl.ds(first, n), at : at + HEAD]
                for ref in key_refs
                for first, n in spans(part)
            ],
            axis=0,
        )

    def tiles(array):
        return [array[:, n : n + HEAD] for n in range(0, keys_step, HEAD)]

    for part in range(clips + 1):
        k_pos = MEMBERS * idx_of(lane % STEP, part) + k_mem
        q_pos = MEMBERS * idx_of(row, part) + member
        allowed = jnp.concatenate([k_pos <= q_pos] * heads, axis=0)
        q = jnp.concatenate(
            [
                q_ref[pl.ds(first, n), h * HEAD : (h + 1) * HEAD]
                for h in range(heads)
                for first, n in spans(part)
            ],
            axis=0,
        )
        scores = []
        for kp in range(part + 1):
            s = lax.dot_general(
                q, gather(kp, 0), (((1,), (1,)), ((), ())), preferred_element_type=jnp.float32
            ) * scale
            if kp == part:
                s = jnp.where(allowed, s, NEG_FILL)
            scores.append(s)
        top = functools.reduce(jnp.maximum, [tile for s in scores for tile in tiles(s)])
        top = jnp.max(top, axis=-1, keepdims=True)
        total, acc = None, None
        for kp, s in enumerate(scores):
            w = jnp.exp2(s - top)
            more = functools.reduce(jnp.add, tiles(w))
            total = more if total is None else total + more
            more = jnp.dot(
                w.astype(jnp.bfloat16), gather(kp, HEAD), preferred_element_type=jnp.float32
            )
            acc = more if acc is None else acc + more
        total = jnp.sum(total, axis=-1, keepdims=True)
        out = (acc / total).astype(jnp.bfloat16)
        for h in range(heads):
            at = slice(h * HEAD, (h + 1) * HEAD)
            if part == clips:
                out_ref[pl.ds(part * STEP, STEP), at] = out[h * STEP : (h + 1) * STEP]
                continue
            for dy in range(GROUPS):
                y = (group + GROUPS - dy) % GROUPS
                to = pl.ds(pl.multiple_of(part * STEP + y * PART, PART), PART)
                first = h * STEP + dy * PART
                out_ref[to, at] = out[first : first + PART]
    _, at = iotas((o_ref.shape[0], out_ref.shape[0]))
    pick = one_hot(at == to_ref[...])
    o_ref[...] = jnp.dot(pick, out_ref[...], preferred_element_type=jnp.float32).astype(
        jnp.bfloat16
    )


def attend(info, q, to, pieces, heads, clips):
    return pl.pallas_call(
        functools.partial(attend_kernel, heads, clips),
        out_shape=jax.ShapeDtypeStruct(q.shape, jnp.bfloat16),
        in_specs=[SMEM_SPEC] + [VMEM_SPEC] * (2 + len(pieces)),
        out_specs=VMEM_SPEC,
        scratch_shapes=[pltpu.VMEM(q.shape, jnp.bfloat16)],
        compiler_params=pltpu.CompilerParams(vmem_limit_bytes=MID_VMEM),
        cost_estimate=pl.CostEstimate(
            flops=1300000000, bytes_accessed=4000000, transcendentals=2500000
        ),
    )(info, q, to, *pieces)


def per_device(
    clip_store,
    text_tokens,
    candidates,
    clip_slot,
    text_positions,
    block_order,
    w_query,
    b_query,
    key_value_weight,
    value_offset_bias,
):
    me = lax.axis_index("ctx")
    plane = lax.axis_index("mp")
    group, member = me // MEMBERS, me % MEMBERS
    core = member % 2
    clips_here, clip_len, feat = clip_store.shape
    seqs, cands = candidates.shape
    text_len = text_positions.shape[1]
    width = w_query.shape[1]
    heads = width // HEAD

    sent = pack(candidates, clip_slot, me, clip_store, text_tokens)
    sent = lax.all_to_all(sent, "ctx", 0, 0, tiled=True)

    kv_flat = key_value_weight.reshape(key_value_weight.shape[0], -1)
    text_at = lax.dynamic_index_in_dim(
        lax.dynamic_index_in_dim(text_positions, group, 0, keepdims=False).reshape(-1, MEMBERS),
        member, 1, keepdims=False,
    )
    clip_idx = STEP * jnp.arange(cands)[:, None] + jnp.arange(PART)[None, :]

    def clip_pos(dy):
        y = (group - dy) % GROUPS
        return (MEMBERS * (clip_idx + PART * y) + member).astype(jnp.int32).reshape(-1)

    cosine, sine = rope_tables(jnp.concatenate([text_at] + [clip_pos(dy) for dy in range(GROUPS)]))
    blocks = block_order.shape[0]
    block_len = (cands * clip_len + text_len) // blocks
    sub = block_len // MEMBERS
    send_from = sub * block_order.reshape(DEVICES, 1, 2) + jnp.arange(sub).reshape(1, sub, 1)
    send_from = send_from.astype(jnp.int32).reshape(-1, 1)
    sent, kv_flat, cosine, sine, send_from = lax.optimization_barrier(
        (sent, kv_flat, cosine, sine, send_from)
    )

    first, *others = unpack(candidates, clip_slot, group, sent, clips_here)
    arrived = [
        lax.ppermute(out, "ctx", ctx_pairs(lambda y, x, c, dy=dy: (y + dy, x, c)))
        for dy, out in enumerate(others, 1)
    ]
    first, arrived[1] = lax.optimization_barrier((first, arrived[1]))
    own = [first, jnp.concatenate(arrived, 0)]

    fwd, bwd = list(own), list(own)
    sums, parts, owners = None, [own], [plane]
    for hop in range(1, PLANES // 2):
        for h in range(len(own)):
            fwd[h] = lax.ppermute(fwd[h], "mp", shifted(PLANES, 1))
            bwd[h] = lax.ppermute(bwd[h], "mp", shifted(PLANES, -1))
        if hop in MULTIPLY_AT:
            sums = add_products(sums, parts, owners, w_query, kv_flat)
            fwd[-1], bwd[-1], sums = lax.optimization_barrier((fwd[-1], bwd[-1], sums))
            parts, owners = [], []
        parts += [list(fwd), list(bwd)]
        owners += [(plane - hop) % PLANES, (plane + hop) % PLANES]
    far = [
        lax.ppermute(jnp.where(core == 0, fwd[h], bwd[h]), ("ctx", "mp"), far_pairs())
        for h in range(len(own))
    ]
    sums = add_products(sums, parts, owners, w_query, kv_flat)
    far[-1], sums = lax.optimization_barrier((far[-1], sums))
    opposite = (plane + PLANES // 2) % PLANES
    kv = finish(True, sums[1], far, opposite, kv_flat, cosine, sine, value_offset_bias)
    q = finish(False, sums[0], far, opposite, w_query, cosine, sine, b_query)

    below = lax.ppermute(kv, "ctx", ctx_pairs(lambda y, x, c: (y, x + 1, c)))
    above = lax.ppermute(kv, "ctx", ctx_pairs(lambda y, x, c: (y, x - 1, c)))
    above, q = lax.optimization_barrier((above, q))
    beyond = lax.ppermute(
        jnp.where(core == 0, above, below), "ctx",
        ctx_pairs(lambda y, x, c: (y, x + (-1 if c == 0 else 1), c)),
    )
    swap = ctx_pairs(lambda y, x, c: (y, x, 1 - c))
    pieces = []
    for piece in (kv, below, above, beyond):
        pieces += [piece, lax.ppermute(piece, "ctx", swap)]

    info = jnp.stack([group, member]).astype(jnp.int32)
    out = attend(info, q, send_from, pieces, heads, cands)

    send = out.reshape(DEVICES, sub, 2, width)
    recv = lax.all_to_all(send, "ctx", 0, 0, tiled=True)
    recv = recv.reshape(GROUPS, MEMBERS, sub, 2, width)
    return recv.transpose(0, 3, 2, 1, 4).reshape(seqs, 2, block_len, width)


def solution(mesh):
    placed = (
        P("ctx", None, "mp"),
        P(None, "ctx", "mp"),
        P(),
        P(),
        P(),
        P(),
        P(None, "mp"),
        P("mp"),
        P(None, None, "mp"),
        P("mp"),
    )
    return jax.shard_map(
        per_device,
        mesh=mesh,
        in_specs=placed,
        out_specs=P(None, "ctx", None, "mp"),
        check_vma=False,
    )
```

```python
import functools
import math

import jax
import jax.numpy as jnp
from jax import lax
from jax.experimental import pallas as pl
from jax.experimental.pallas import tpu as pltpu
from jax.sharding import PartitionSpec as P

HEAD = 128
NEG_FILL = -1e30
ROPE_BASE = 1000000.0
GROUPS = 4
MEMBERS = 8
DEVICES = GROUPS * MEMBERS
PLANES = 8
MULTIPLY_AT = (1, 2, 3)
STEP = 64
PART = 16
TEXT = 2
SMALL_VMEM = 16 * 1024 * 1024
MID_VMEM = 24 * 1024 * 1024
VMEM_SPEC = pl.BlockSpec(memory_space=pltpu.VMEM)
SMEM_SPEC = pl.BlockSpec(memory_space=pltpu.SMEM)
HBM_SPEC = pl.BlockSpec(memory_space=pltpu.HBM)


def in_hbm(*arrays):
    return [pltpu.with_memory_space_constraint(array, pltpu.HBM) for array in arrays]


def shifted(n, by):
    return [(i, (i + by) % n) for i in range(n)]


def ctx_pairs(move):
    pairs = []
    for i in range(DEVICES):
        y, x, c = move(i // MEMBERS, (i // 2) % 4, i % 2)
        pairs.append((i, (y % 4) * MEMBERS + (x % 4) * 2 + c))
    return pairs


def far_pairs():
    return [
        (i * PLANES + z, i * PLANES + (z + (1 if i % 2 == 0 else -1)) % PLANES)
        for i in range(DEVICES)
        for z in range(PLANES)
    ]


def rope_tables(positions):
    half = HEAD // 2
    frequency = ROPE_BASE ** (-(jnp.arange(half, dtype=jnp.float32) * 2.0) / HEAD)
    angles = positions.astype(jnp.float32)[:, None] * frequency
    cosine, sine = jnp.cos(angles), jnp.sin(angles)
    return jnp.concatenate([cosine, cosine], -1), jnp.concatenate([-sine, sine], -1)


def rows_of(refs):
    return refs[0][...] if len(refs) == 1 else jnp.concatenate([r[...] for r in refs], axis=0)


def products_kernel(groups, halves, fresh, owners_ref, wq_hbm, wk_hbm, *refs):
    wq_ref, wk_ref, sems = refs[-3:]
    q_out, k_out = refs[-5:-3]
    feat = wq_ref.shape[1]
    copies = []
    for i in range(groups):
        at = pl.ds(pl.multiple_of(owners_ref[i] * feat, feat), feat)
        for n, (src, dst) in enumerate(((wq_hbm, wq_ref), (wk_hbm, wk_ref))):
            copy = pltpu.make_async_copy(src.at[at, :], dst.at[i], sems.at[n, i])
            copy.start()
            copies.append(copy)
    q = None if fresh else refs[-7][...]
    k = None if fresh else refs[-6][...]
    for i in range(groups):
        copies[2 * i].wait()
        copies[2 * i + 1].wait()
        rows = rows_of(refs[i * halves : (i + 1) * halves])
        more_q = jnp.dot(rows, wq_ref[i], preferred_element_type=jnp.float32)
        more_k = jnp.dot(rows, wk_ref[i], preferred_element_type=jnp.float32)
        q = more_q if q is None else q + more_q
        k = more_k if k is None else k + more_k
    q_out[...] = q
    k_out[...] = k


def add_products(sums, parts, owners, w_query, kv_flat):
    halves, groups = len(parts[0]), len(parts)
    feat = parts[0][0].shape[1]
    count = sum(part.shape[0] for part in parts[0])
    q_cols, k_cols = w_query.shape[1], kv_flat.shape[1]
    args = sum(parts, []) + list(sums or ())
    return pl.pallas_call(
        functools.partial(products_kernel, groups, halves, sums is None),
        in_specs=[SMEM_SPEC, HBM_SPEC, HBM_SPEC] + [VMEM_SPEC] * len(args),
        out_specs=[VMEM_SPEC] * 2,
        out_shape=[
            jax.ShapeDtypeStruct((count, q_cols), jnp.float32),
            jax.ShapeDtypeStruct((count, k_cols), jnp.float32),
        ],
        scratch_shapes=[
            pltpu.VMEM((groups, feat, q_cols), jnp.bfloat16),
            pltpu.VMEM((groups, feat, k_cols), jnp.bfloat16),
            pltpu.SemaphoreType.DMA((2, groups)),
        ],
        compiler_params=pltpu.CompilerParams(vmem_limit_bytes=SMALL_VMEM),
        cost_estimate=pl.CostEstimate(
            flops=4 * groups * count * feat * (q_cols + k_cols),
            bytes_accessed=groups * feat * (q_cols + k_cols) * 2,
            transcendentals=0,
        ),
    )(jnp.stack(owners).astype(jnp.int32), *in_hbm(w_query, kv_flat), *args)


def rotated(x, cosine, sine):
    return (x * cosine + pltpu.roll(x, HEAD // 2, 1) * sine).astype(jnp.bfloat16)


def keys_kernel(halves, *refs):
    w_ref, sum_ref, cos_ref, sin_ref, bias_ref, o_ref = refs[halves:]
    rows = rows_of(refs[:halves])
    out = sum_ref[...] + jnp.dot(rows, w_ref[...], preferred_element_type=jnp.float32)
    o_ref[:, :HEAD] = rotated(out[:, :HEAD], cos_ref[...], sin_ref[...])
    o_ref[:, HEAD:] = (out[:, HEAD:] + bias_ref[...].astype(jnp.float32)).astype(jnp.bfloat16)


def finish_keys(total, far, weight, cosine, sine, bias):
    args = [*far, weight, total, cosine, sine, bias.reshape(1, -1)]
    return pl.pallas_call(
        functools.partial(keys_kernel, len(far)),
        in_specs=[VMEM_SPEC] * len(args),
        out_specs=VMEM_SPEC,
        out_shape=jax.ShapeDtypeStruct(total.shape, jnp.bfloat16),
        compiler_params=pltpu.CompilerParams(vmem_limit_bytes=SMALL_VMEM),
    )(*args)


def finish_kernel(halves, owner_ref, w_hbm, *refs):
    sum_ref, cos_ref, sin_ref, bias_ref, o_ref, w_ref, sem = refs[halves:]
    feat = w_ref.shape[0]
    at = pl.ds(pl.multiple_of(owner_ref[0] * feat, feat), feat)
    copy = pltpu.make_async_copy(w_hbm.at[at, :], w_ref, sem)
    copy.start()
    rows = rows_of(refs[:halves])
    copy.wait()
    out = sum_ref[...] + jnp.dot(rows, w_ref[...], preferred_element_type=jnp.float32)
    out = out + bias_ref[...].astype(jnp.float32)
    for h in range(out.shape[1] // HEAD):
        at = slice(h * HEAD, (h + 1) * HEAD)
        o_ref[:, at] = rotated(out[:, at], cos_ref[...], sin_ref[...])


def finish_queries(total, far, owner, weight, cosine, sine, bias):
    (count, cols), feat = total.shape, far[0].shape[1]
    args = [*far, total, cosine, sine, bias.reshape(1, -1)]
    return pl.pallas_call(
        functools.partial(finish_kernel, len(far)),
        in_specs=[SMEM_SPEC, HBM_SPEC] + [VMEM_SPEC] * len(args),
        out_specs=VMEM_SPEC,
        out_shape=jax.ShapeDtypeStruct((count, cols), jnp.bfloat16),
        scratch_shapes=[pltpu.VMEM((feat, cols), jnp.bfloat16), pltpu.SemaphoreType.DMA],
        compiler_params=pltpu.CompilerParams(vmem_limit_bytes=SMALL_VMEM),
        cost_estimate=pl.CostEstimate(
            flops=4 * count * feat * cols, bytes_accessed=2000000, transcendentals=0
        ),
    )(owner.reshape(1).astype(jnp.int32), *in_hbm(weight), *args)


def one_hot(hit):
    return jnp.where(hit, 1.0, 0.0).astype(jnp.bfloat16)


def iotas(shape):
    return lax.broadcasted_iota(jnp.int32, shape, 0), lax.broadcasted_iota(jnp.int32, shape, 1)


def pack_kernel(clips_here, cand_ref, slot_ref, me_ref, clip_hbm, text_ref, o_ref, held_ref, sem):
    me = me_ref[0]
    which = jnp.int32(0)
    for s in range(cand_ref.shape[0]):
        for k in range(cand_ref.shape[1]):
            slot = slot_ref[cand_ref[s, k]]
            which = jnp.where(slot // clips_here == me, slot % clips_here, which)
    copy = pltpu.make_async_copy(clip_hbm.at[which], held_ref, sem)
    copy.start()
    feat = held_ref.shape[1]
    folds = feat // HEAD
    rows = PART * MEMBERS
    to, at = iotas((rows, PART))
    m, r = to // PART, to % PART
    for y in range(GROUPS):
        text = text_ref[y]
        beside = jnp.zeros((rows, HEAD), jnp.float32)
        for fold in range(folds):
            hit = (r % folds == fold) & (r < TEXT * folds) & (at == m + MEMBERS * (r // folds))
            beside = beside + jnp.dot(
                one_hot(hit), text[:, fold * HEAD : (fold + 1) * HEAD],
                preferred_element_type=jnp.float32,
            )
        o_ref[pl.ds(y * MEMBERS, MEMBERS), :, feat:] = beside.astype(jnp.bfloat16).reshape(
            MEMBERS, PART, HEAD
        )
    to, at = iotas((rows, rows))
    pick = one_hot(at == MEMBERS * (to % PART) + to // PART)
    copy.wait()
    for y in range(GROUPS):
        out = jnp.dot(pick, held_ref[rows * y : rows * (y + 1)], preferred_element_type=jnp.float32)
        o_ref[pl.ds(y * MEMBERS, MEMBERS), :, :feat] = out.astype(jnp.bfloat16).reshape(
            MEMBERS, PART, feat
        )


def pack(candidates, clip_slot, me, clip_store, text_tokens):
    clips_here, clip_len, feat = clip_store.shape
    return pl.pallas_call(
        functools.partial(pack_kernel, clips_here),
        out_shape=jax.ShapeDtypeStruct((DEVICES, PART, feat + HEAD), jnp.bfloat16),
        in_specs=[SMEM_SPEC] * 3 + [HBM_SPEC, VMEM_SPEC],
        out_specs=VMEM_SPEC,
        scratch_shapes=[pltpu.VMEM((clip_len, feat), jnp.bfloat16), pltpu.SemaphoreType.DMA],
        compiler_params=pltpu.CompilerParams(vmem_limit_bytes=SMALL_VMEM),
    )(*in_hbm(candidates, clip_slot), me.reshape(1).astype(jnp.int32), *in_hbm(clip_store, text_tokens))


def unpack_kernel(clips_here, cand_ref, slot_ref, group_ref, sent_ref, own_ref, *out_refs):
    group = group_ref[0]
    feat = own_ref.shape[1]
    folds = feat // HEAD
    beside = sent_ref[:, :, feat:].reshape(DEVICES * PART, HEAD)
    to, at = iotas((TEXT * DEVICES, DEVICES * PART))
    for fold in range(folds):
        hit = at == (to // TEXT) * PART + (to % TEXT) * folds + fold
        own_ref[:STEP, fold * HEAD : (fold + 1) * HEAD] = jnp.dot(
            one_hot(hit), beside, preferred_element_type=jnp.float32
        ).astype(jnp.bfloat16)
    cands = cand_ref.shape[1]
    for dy in range(GROUPS):
        seq = (group + dy) % GROUPS
        for k in range(cands):
            source = slot_ref[cand_ref[seq, k]] // clips_here
            rows = sent_ref[source, :, :feat]
            if dy == 0:
                own_ref[STEP + PART * k : STEP + PART * (k + 1)] = rows
            else:
                out_refs[dy - 1][PART * k : PART * (k + 1)] = rows


def unpack(candidates, clip_slot, group, sent, clips_here):
    feat = sent.shape[2] - HEAD
    shapes = [(2 * STEP, feat)] + [(STEP, feat)] * (GROUPS - 1)
    return pl.pallas_call(
        functools.partial(unpack_kernel, clips_here),
        out_shape=[jax.ShapeDtypeStruct(s, jnp.bfloat16) for s in shapes],
        in_specs=[SMEM_SPEC] * 3 + [VMEM_SPEC],
        out_specs=[VMEM_SPEC] * GROUPS,
        compiler_params=pltpu.CompilerParams(vmem_limit_bytes=SMALL_VMEM),
    )(*in_hbm(candidates, clip_slot), group.reshape(1).astype(jnp.int32), sent)


def attend_kernel(heads, clips, info_ref, q_ref, to_ref, *refs):
    o_ref, out_ref, key_refs = refs[-2], refs[-1], refs[:-2]
    group, member = info_ref[0], info_ref[1]
    my_x, my_core = member // 2, member % 2
    scale = math.log2(math.e) / math.sqrt(HEAD)

    def spans(part):
        if part == clips:
            return [(0, STEP)]
        return [(STEP + dy * STEP + PART * part, PART) for dy in range(GROUPS)]

    def idx_of(row, part):
        if part == clips:
            return row
        return ((group + GROUPS - row // PART) % GROUPS) * PART + row % PART

    keys_step = MEMBERS * STEP
    lane = lax.broadcasted_iota(jnp.int32, (STEP, keys_step), 1)
    row = lax.broadcasted_iota(jnp.int32, (STEP, keys_step), 0)
    slot = lane // STEP
    pair = slot // 2
    off = jnp.where(pair == 0, 0, jnp.where(pair == 1, 3, pair - 1))
    k_mem = 2 * ((my_x + off) % 4) + (my_core + slot) % 2

    def gather(part, at):
        return jnp.concatenate(
            [
                ref[pl.ds(first, n), at : at + HEAD]
                for ref in key_refs
                for first, n in spans(part)
            ],
            axis=0,
        )

    def tiles(array):
        return [array[:, n : n + HEAD] for n in range(0, keys_step, HEAD)]

    for part in range(clips + 1):
        k_pos = MEMBERS * idx_of(lane % STEP, part) + k_mem
        q_pos = MEMBERS * idx_of(row, part) + member
        allowed = jnp.concatenate([k_pos <= q_pos] * heads, axis=0)
        q = jnp.concatenate(
            [
                q_ref[pl.ds(first, n), h * HEAD : (h + 1) * HEAD]
                for h in range(heads)
                for first, n in spans(part)
            ],
            axis=0,
        )
        scores = []
        for kp in range(part + 1):
            s = lax.dot_general(
                q, gather(kp, 0), (((1,), (1,)), ((), ())), preferred_element_type=jnp.float32
            ) * scale
            if kp == part:
                s = jnp.where(allowed, s, NEG_FILL)
            scores.append(s)
        top = functools.reduce(jnp.maximum, [tile for s in scores for tile in tiles(s)])
        top = jnp.max(top, axis=-1, keepdims=True)
        total, acc = None, None
        for kp, s in enumerate(scores):
            w = jnp.exp2(s - top)
            more = functools.reduce(jnp.add, tiles(w))
            total = more if total is None else total + more
            more = jnp.dot(
                w.astype(jnp.bfloat16), gather(kp, HEAD), preferred_element_type=jnp.float32
            )
            acc = more if acc is None else acc + more
        total = jnp.sum(total, axis=-1, keepdims=True)
        out = (acc / total).astype(jnp.bfloat16)
        for h in range(heads):
            at = slice(h * HEAD, (h + 1) * HEAD)
            if part == clips:
                out_ref[pl.ds(part * STEP, STEP), at] = out[h * STEP : (h + 1) * STEP]
                continue
            for dy in range(GROUPS):
                y = (group + GROUPS - dy) % GROUPS
                to = pl.ds(pl.multiple_of(part * STEP + y * PART, PART), PART)
                first = h * STEP + dy * PART
                out_ref[to, at] = out[first : first + PART]
    _, at = iotas((o_ref.shape[0], out_ref.shape[0]))
    pick = one_hot(at == to_ref[...])
    o_ref[...] = jnp.dot(pick, out_ref[...], preferred_element_type=jnp.float32).astype(
        jnp.bfloat16
    )


def attend(info, q, to, pieces, heads, clips):
    return pl.pallas_call(
        functools.partial(attend_kernel, heads, clips),
        out_shape=jax.ShapeDtypeStruct(q.shape, jnp.bfloat16),
        in_specs=[SMEM_SPEC] + [VMEM_SPEC] * (2 + len(pieces)),
        out_specs=VMEM_SPEC,
        scratch_shapes=[pltpu.VMEM(q.shape, jnp.bfloat16)],
        compiler_params=pltpu.CompilerParams(vmem_limit_bytes=MID_VMEM),
        cost_estimate=pl.CostEstimate(
            flops=1300000000, bytes_accessed=4000000, transcendentals=2500000
        ),
    )(info, q, to, *pieces)


def per_device(
    clip_store,
    text_tokens,
    candidates,
    clip_slot,
    text_positions,
    block_order,
    w_query,
    b_query,
    key_value_weight,
    value_offset_bias,
):
    me = lax.axis_index("ctx")
    plane = lax.axis_index("mp")
    group, member = me // MEMBERS, me % MEMBERS
    core = member % 2
    clips_here, clip_len, feat = clip_store.shape
    seqs, cands = candidates.shape
    text_len = text_positions.shape[1]
    width = w_query.shape[1]
    heads = width // HEAD

    sent = pack(candidates, clip_slot, me, clip_store, text_tokens)
    sent = lax.all_to_all(sent, "ctx", 0, 0, tiled=True)

    kv_flat = key_value_weight.reshape(key_value_weight.shape[0], -1)
    opposite = (plane + PLANES // 2) % PLANES
    kv_opposite = lax.dynamic_slice_in_dim(kv_flat, opposite * feat, feat, 0)
    text_at = lax.dynamic_index_in_dim(
        lax.dynamic_index_in_dim(text_positions, group, 0, keepdims=False).reshape(-1, MEMBERS),
        member, 1, keepdims=False,
    )
    clip_idx = STEP * jnp.arange(cands)[:, None] + jnp.arange(PART)[None, :]

    def clip_pos(dy):
        y = (group - dy) % GROUPS
        return (MEMBERS * (clip_idx + PART * y) + member).astype(jnp.int32).reshape(-1)

    cosine, sine = rope_tables(jnp.concatenate([text_at] + [clip_pos(dy) for dy in range(GROUPS)]))
    blocks = block_order.shape[0]
    block_len = (cands * clip_len + text_len) // blocks
    sub = block_len // MEMBERS
    send_from = sub * block_order.reshape(DEVICES, 1, 2) + jnp.arange(sub).reshape(1, sub, 1)
    send_from = send_from.astype(jnp.int32).reshape(-1, 1)
    sent, kv_flat, kv_opposite, cosine, sine, send_from = lax.optimization_barrier(
        (sent, kv_flat, kv_opposite, cosine, sine, send_from)
    )

    first, *others = unpack(candidates, clip_slot, group, sent, clips_here)
    arrived = [
        lax.ppermute(out, "ctx", ctx_pairs(lambda y, x, c, dy=dy: (y + dy, x, c)))
        for dy, out in enumerate(others, 1)
    ]
    first, arrived[1] = lax.optimization_barrier((first, arrived[1]))
    own = [first, jnp.concatenate(arrived, 0)]

    fwd, bwd = list(own), list(own)
    sums, parts, owners = None, [own], [plane]
    for hop in range(1, PLANES // 2):
        for h in range(len(own)):
            fwd[h] = lax.ppermute(fwd[h], "mp", shifted(PLANES, 1))
            bwd[h] = lax.ppermute(bwd[h], "mp", shifted(PLANES, -1))
        if hop in MULTIPLY_AT:
            sums = add_products(sums, parts, owners, w_query, kv_flat)
            fwd[-1], bwd[-1], sums = lax.optimization_barrier((fwd[-1], bwd[-1], sums))
            parts, owners = [], []
        parts += [list(fwd), list(bwd)]
        owners += [(plane - hop) % PLANES, (plane + hop) % PLANES]
    far = [
        lax.ppermute(jnp.where(core == 0, fwd[h], bwd[h]), ("ctx", "mp"), far_pairs())
        for h in range(len(own))
    ]
    sums = add_products(sums, parts, owners, w_query, kv_flat)
    far[-1], sums = lax.optimization_barrier((far[-1], sums))
    kv = finish_keys(sums[1], far, kv_opposite, cosine, sine, value_offset_bias)
    q = finish_queries(sums[0], far, opposite, w_query, cosine, sine, b_query)

    below = lax.ppermute(kv, "ctx", ctx_pairs(lambda y, x, c: (y, x + 1, c)))
    above = lax.ppermute(kv, "ctx", ctx_pairs(lambda y, x, c: (y, x - 1, c)))
    swap = ctx_pairs(lambda y, x, c: (y, x, 1 - c))
    beside = lax.ppermute(kv, "ctx", swap)
    above, beside, q = lax.optimization_barrier((above, beside, q))
    beyond = lax.ppermute(
        jnp.where(core == 0, above, below), "ctx",
        ctx_pairs(lambda y, x, c: (y, x + (-1 if c == 0 else 1), c)),
    )
    pieces = [kv, beside]
    for piece in (below, above, beyond):
        pieces += [piece, lax.ppermute(piece, "ctx", swap)]

    info = jnp.stack([group, member]).astype(jnp.int32)
    out = attend(info, q, send_from, pieces, heads, cands)

    send = out.reshape(DEVICES, sub, 2, width)
    recv = lax.all_to_all(send, "ctx", 0, 0, tiled=True)
    recv = recv.reshape(GROUPS, MEMBERS, sub, 2, width)
    return recv.transpose(0, 3, 2, 1, 4).reshape(seqs, 2, block_len, width)


def solution(mesh):
    placed = (
        P("ctx", None, "mp"),
        P(None, "ctx", "mp"),
        P(),
        P(),
        P(),
        P(),
        P(None, "mp"),
        P("mp"),
        P(None, None, "mp"),
        P("mp"),
    )
    return jax.shard_map(
        per_device,
        mesh=mesh,
        in_specs=placed,
        out_specs=P(None, "ctx", None, "mp"),
        check_vma=False,
    )
```

```python
import functools
import math

import jax
import jax.numpy as jnp
from jax import lax
from jax.experimental import pallas as pl
from jax.experimental.pallas import tpu as pltpu
from jax.sharding import PartitionSpec as P

HEAD = 128
NEG_FILL = -1e30
ROPE_BASE = 1000000.0
GROUPS = 4
MEMBERS = 8
DEVICES = GROUPS * MEMBERS
PLANES = 8
MULTIPLY_AT = (1, 2, 3)
STEP = 64
PART = 16
TEXT = 2
SMALL_VMEM = 16 * 1024 * 1024
MID_VMEM = 24 * 1024 * 1024
VMEM_SPEC = pl.BlockSpec(memory_space=pltpu.VMEM)
SMEM_SPEC = pl.BlockSpec(memory_space=pltpu.SMEM)
HBM_SPEC = pl.BlockSpec(memory_space=pltpu.HBM)


def in_hbm(*arrays):
    return [pltpu.with_memory_space_constraint(array, pltpu.HBM) for array in arrays]


def shifted(n, by):
    return [(i, (i + by) % n) for i in range(n)]


def ctx_pairs(move):
    pairs = []
    for i in range(DEVICES):
        y, x, c = move(i // MEMBERS, (i // 2) % 4, i % 2)
        pairs.append((i, (y % 4) * MEMBERS + (x % 4) * 2 + c))
    return pairs


def far_pairs():
    return [
        (i * PLANES + z, i * PLANES + (z + (1 if i % 2 == 0 else -1)) % PLANES)
        for i in range(DEVICES)
        for z in range(PLANES)
    ]


def rope_tables(positions):
    half = HEAD // 2
    frequency = ROPE_BASE ** (-(jnp.arange(half, dtype=jnp.float32) * 2.0) / HEAD)
    angles = positions.astype(jnp.float32)[:, None] * frequency
    cosine, sine = jnp.cos(angles), jnp.sin(angles)
    return jnp.concatenate([cosine, cosine], -1), jnp.concatenate([-sine, sine], -1)


def rows_of(refs):
    return refs[0][...] if len(refs) == 1 else jnp.concatenate([r[...] for r in refs], axis=0)


def products_kernel(groups, halves, fresh, owners_ref, wq_hbm, wk_hbm, *refs):
    wq_ref, wk_ref, sems = refs[-3:]
    q_out, k_out = refs[-5:-3]
    feat = wq_ref.shape[1]
    copies = []
    for i in range(groups):
        at = pl.ds(pl.multiple_of(owners_ref[i] * feat, feat), feat)
        for n, (src, dst) in enumerate(((wq_hbm, wq_ref), (wk_hbm, wk_ref))):
            copy = pltpu.make_async_copy(src.at[at, :], dst.at[i], sems.at[n, i])
            copy.start()
            copies.append(copy)
    q = None if fresh else refs[-7][...]
    k = None if fresh else refs[-6][...]
    for i in range(groups):
        copies[2 * i].wait()
        copies[2 * i + 1].wait()
        rows = rows_of(refs[i * halves : (i + 1) * halves])
        more_q = jnp.dot(rows, wq_ref[i], preferred_element_type=jnp.float32)
        more_k = jnp.dot(rows, wk_ref[i], preferred_element_type=jnp.float32)
        q = more_q if q is None else q + more_q
        k = more_k if k is None else k + more_k
    q_out[...] = q
    k_out[...] = k


def add_products(sums, parts, owners, w_query, kv_flat):
    halves, groups = len(parts[0]), len(parts)
    feat = parts[0][0].shape[1]
    count = sum(part.shape[0] for part in parts[0])
    q_cols, k_cols = w_query.shape[1], kv_flat.shape[1]
    args = sum(parts, []) + list(sums or ())
    return pl.pallas_call(
        functools.partial(products_kernel, groups, halves, sums is None),
        in_specs=[SMEM_SPEC, HBM_SPEC, HBM_SPEC] + [VMEM_SPEC] * len(args),
        out_specs=[VMEM_SPEC] * 2,
        out_shape=[
            jax.ShapeDtypeStruct((count, q_cols), jnp.float32),
            jax.ShapeDtypeStruct((count, k_cols), jnp.float32),
        ],
        scratch_shapes=[
            pltpu.VMEM((groups, feat, q_cols), jnp.bfloat16),
            pltpu.VMEM((groups, feat, k_cols), jnp.bfloat16),
            pltpu.SemaphoreType.DMA((2, groups)),
        ],
        compiler_params=pltpu.CompilerParams(vmem_limit_bytes=SMALL_VMEM),
        cost_estimate=pl.CostEstimate(
            flops=4 * groups * count * feat * (q_cols + k_cols),
            bytes_accessed=groups * feat * (q_cols + k_cols) * 2,
            transcendentals=0,
        ),
    )(jnp.stack(owners).astype(jnp.int32), *in_hbm(w_query, kv_flat), *args)


def rotated(x, cosine, sine):
    return (x * cosine + pltpu.roll(x, HEAD // 2, 1) * sine).astype(jnp.bfloat16)


def keys_kernel(halves, *refs):
    w_ref, sum_ref, cos_ref, sin_ref, bias_ref, o_ref = refs[halves:]
    rows = rows_of(refs[:halves])
    out = sum_ref[...] + jnp.dot(rows, w_ref[...], preferred_element_type=jnp.float32)
    o_ref[:, :HEAD] = rotated(out[:, :HEAD], cos_ref[...], sin_ref[...])
    o_ref[:, HEAD:] = (out[:, HEAD:] + bias_ref[...].astype(jnp.float32)).astype(jnp.bfloat16)


def finish_keys(total, far, weight, cosine, sine, bias):
    args = [*far, weight, total, cosine, sine, bias.reshape(1, -1)]
    return pl.pallas_call(
        functools.partial(keys_kernel, len(far)),
        in_specs=[VMEM_SPEC] * len(args),
        out_specs=VMEM_SPEC,
        out_shape=jax.ShapeDtypeStruct(total.shape, jnp.bfloat16),
        compiler_params=pltpu.CompilerParams(vmem_limit_bytes=SMALL_VMEM),
    )(*args)


def finish_kernel(halves, owner_ref, w_hbm, *refs):
    sum_ref, cos_ref, sin_ref, bias_ref, o_ref, w_ref, sem = refs[halves:]
    feat = w_ref.shape[0]
    at = pl.ds(pl.multiple_of(owner_ref[0] * feat, feat), feat)
    copy = pltpu.make_async_copy(w_hbm.at[at, :], w_ref, sem)
    copy.start()
    rows = rows_of(refs[:halves])
    copy.wait()
    out = sum_ref[...] + jnp.dot(rows, w_ref[...], preferred_element_type=jnp.float32)
    out = out + bias_ref[...].astype(jnp.float32)
    for h in range(out.shape[1] // HEAD):
        at = slice(h * HEAD, (h + 1) * HEAD)
        o_ref[:, at] = rotated(out[:, at], cos_ref[...], sin_ref[...])


def finish_queries(total, far, owner, weight, cosine, sine, bias):
    (count, cols), feat = total.shape, far[0].shape[1]
    args = [*far, total, cosine, sine, bias.reshape(1, -1)]
    return pl.pallas_call(
        functools.partial(finish_kernel, len(far)),
        in_specs=[SMEM_SPEC, HBM_SPEC] + [VMEM_SPEC] * len(args),
        out_specs=VMEM_SPEC,
        out_shape=jax.ShapeDtypeStruct((count, cols), jnp.bfloat16),
        scratch_shapes=[pltpu.VMEM((feat, cols), jnp.bfloat16), pltpu.SemaphoreType.DMA],
        compiler_params=pltpu.CompilerParams(vmem_limit_bytes=SMALL_VMEM),
        cost_estimate=pl.CostEstimate(
            flops=4 * count * feat * cols, bytes_accessed=2000000, transcendentals=0
        ),
    )(owner.reshape(1).astype(jnp.int32), *in_hbm(weight), *args)


def one_hot(hit):
    return jnp.where(hit, 1.0, 0.0).astype(jnp.bfloat16)


def iotas(shape):
    return lax.broadcasted_iota(jnp.int32, shape, 0), lax.broadcasted_iota(jnp.int32, shape, 1)


def pack_kernel(clips_here, cand_ref, slot_ref, me_ref, clip_hbm, text_ref, o_ref, held_ref, sem):
    me = me_ref[0]
    which = jnp.int32(0)
    for s in range(cand_ref.shape[0]):
        for k in range(cand_ref.shape[1]):
            slot = slot_ref[cand_ref[s, k]]
            which = jnp.where(slot // clips_here == me, slot % clips_here, which)
    copy = pltpu.make_async_copy(clip_hbm.at[which], held_ref, sem)
    copy.start()
    feat = held_ref.shape[1]
    folds = feat // HEAD
    rows = PART * MEMBERS
    to, at = iotas((rows, PART))
    m, r = to // PART, to % PART
    for y in range(GROUPS):
        text = text_ref[y]
        beside = jnp.zeros((rows, HEAD), jnp.float32)
        for fold in range(folds):
            hit = (r % folds == fold) & (r < TEXT * folds) & (at == m + MEMBERS * (r // folds))
            beside = beside + jnp.dot(
                one_hot(hit), text[:, fold * HEAD : (fold + 1) * HEAD],
                preferred_element_type=jnp.float32,
            )
        o_ref[pl.ds(y * MEMBERS, MEMBERS), :, feat:] = beside.astype(jnp.bfloat16).reshape(
            MEMBERS, PART, HEAD
        )
    to, at = iotas((rows, rows))
    pick = one_hot(at == MEMBERS * (to % PART) + to // PART)
    copy.wait()
    for y in range(GROUPS):
        out = jnp.dot(pick, held_ref[rows * y : rows * (y + 1)], preferred_element_type=jnp.float32)
        o_ref[pl.ds(y * MEMBERS, MEMBERS), :, :feat] = out.astype(jnp.bfloat16).reshape(
            MEMBERS, PART, feat
        )


def pack(candidates, clip_slot, me, clip_store, text_tokens):
    clips_here, clip_len, feat = clip_store.shape
    return pl.pallas_call(
        functools.partial(pack_kernel, clips_here),
        out_shape=jax.ShapeDtypeStruct((DEVICES, PART, feat + HEAD), jnp.bfloat16),
        in_specs=[SMEM_SPEC] * 3 + [HBM_SPEC, VMEM_SPEC],
        out_specs=VMEM_SPEC,
        scratch_shapes=[pltpu.VMEM((clip_len, feat), jnp.bfloat16), pltpu.SemaphoreType.DMA],
        compiler_params=pltpu.CompilerParams(vmem_limit_bytes=SMALL_VMEM),
    )(*in_hbm(candidates, clip_slot), me.reshape(1).astype(jnp.int32), *in_hbm(clip_store, text_tokens))


def unpack_kernel(clips_here, cand_ref, slot_ref, group_ref, sent_ref, own_ref, *out_refs):
    group = group_ref[0]
    feat = own_ref.shape[1]
    folds = feat // HEAD
    beside = sent_ref[:, :, feat:].reshape(DEVICES * PART, HEAD)
    to, at = iotas((TEXT * DEVICES, DEVICES * PART))
    for fold in range(folds):
        hit = at == (to // TEXT) * PART + (to % TEXT) * folds + fold
        own_ref[:STEP, fold * HEAD : (fold + 1) * HEAD] = jnp.dot(
            one_hot(hit), beside, preferred_element_type=jnp.float32
        ).astype(jnp.bfloat16)
    cands = cand_ref.shape[1]
    for dy in range(GROUPS):
        seq = (group + dy) % GROUPS
        for k in range(cands):
            source = slot_ref[cand_ref[seq, k]] // clips_here
            rows = sent_ref[source, :, :feat]
            if dy == 0:
                own_ref[STEP + PART * k : STEP + PART * (k + 1)] = rows
            else:
                out_refs[dy - 1][PART * k : PART * (k + 1)] = rows


def unpack(candidates, clip_slot, group, sent, clips_here):
    feat = sent.shape[2] - HEAD
    shapes = [(2 * STEP, feat)] + [(STEP, feat)] * (GROUPS - 1)
    return pl.pallas_call(
        functools.partial(unpack_kernel, clips_here),
        out_shape=[jax.ShapeDtypeStruct(s, jnp.bfloat16) for s in shapes],
        in_specs=[SMEM_SPEC] * 3 + [VMEM_SPEC],
        out_specs=[VMEM_SPEC] * GROUPS,
        compiler_params=pltpu.CompilerParams(vmem_limit_bytes=SMALL_VMEM),
    )(*in_hbm(candidates, clip_slot), group.reshape(1).astype(jnp.int32), sent)


def attend_kernel(heads, clips, info_ref, q_ref, to_ref, *refs):
    o_ref, out_ref, key_refs = refs[-2], refs[-1], refs[:-2]
    group, member = info_ref[0], info_ref[1]
    my_x, my_core = member // 2, member % 2
    scale = math.log2(math.e) / math.sqrt(HEAD)

    def spans(part):
        if part == clips:
            return [(0, STEP)]
        return [(STEP + dy * STEP + PART * part, PART) for dy in range(GROUPS)]

    def idx_of(row, part):
        if part == clips:
            return row
        return ((group + GROUPS - row // PART) % GROUPS) * PART + row % PART

    keys_step = MEMBERS * STEP
    lane = lax.broadcasted_iota(jnp.int32, (STEP, keys_step), 1)
    row = lax.broadcasted_iota(jnp.int32, (STEP, keys_step), 0)
    slot = lane // STEP
    pair = slot // 2
    off = jnp.where(pair == 0, 0, jnp.where(pair == 1, 3, pair - 1))
    k_mem = 2 * ((my_x + off) % 4) + (my_core + slot) % 2

    def gather(part, at):
        return jnp.concatenate(
            [
                ref[pl.ds(first, n), at : at + HEAD]
                for ref in key_refs
                for first, n in spans(part)
            ],
            axis=0,
        )

    def tiles(array):
        return [array[:, n : n + HEAD] for n in range(0, keys_step, HEAD)]

    for part in range(clips + 1):
        k_pos = MEMBERS * idx_of(lane % STEP, part) + k_mem
        q_pos = MEMBERS * idx_of(row, part) + member
        allowed = jnp.concatenate([k_pos <= q_pos] * heads, axis=0)
        q = jnp.concatenate(
            [
                q_ref[pl.ds(first, n), h * HEAD : (h + 1) * HEAD]
                for h in range(heads)
                for first, n in spans(part)
            ],
            axis=0,
        )
        scores = []
        for kp in range(part + 1):
            s = lax.dot_general(
                q, gather(kp, 0), (((1,), (1,)), ((), ())), preferred_element_type=jnp.float32
            ) * scale
            if kp == part:
                s = jnp.where(allowed, s, NEG_FILL)
            scores.append(s)
        top = functools.reduce(jnp.maximum, [tile for s in scores for tile in tiles(s)])
        top = jnp.max(top, axis=-1, keepdims=True)
        total, acc = None, None
        for kp, s in enumerate(scores):
            w = jnp.exp2(s - top)
            more = functools.reduce(jnp.add, tiles(w))
            total = more if total is None else total + more
            more = jnp.dot(
                w.astype(jnp.bfloat16), gather(kp, HEAD), preferred_element_type=jnp.float32
            )
            acc = more if acc is None else acc + more
        total = jnp.sum(total, axis=-1, keepdims=True)
        out = (acc / total).astype(jnp.bfloat16)
        for h in range(heads):
            at = slice(h * HEAD, (h + 1) * HEAD)
            if part == clips:
                out_ref[pl.ds(part * STEP, STEP), at] = out[h * STEP : (h + 1) * STEP]
                continue
            for dy in range(GROUPS):
                y = (group + GROUPS - dy) % GROUPS
                to = pl.ds(pl.multiple_of(part * STEP + y * PART, PART), PART)
                first = h * STEP + dy * PART
                out_ref[to, at] = out[first : first + PART]
    _, at = iotas((o_ref.shape[0], out_ref.shape[0]))
    pick = one_hot(at == to_ref[...])
    o_ref[...] = jnp.dot(pick, out_ref[...], preferred_element_type=jnp.float32).astype(
        jnp.bfloat16
    )


def attend(info, q, to, pieces, heads, clips):
    return pl.pallas_call(
        functools.partial(attend_kernel, heads, clips),
        out_shape=jax.ShapeDtypeStruct(q.shape, jnp.bfloat16),
        in_specs=[SMEM_SPEC] + [VMEM_SPEC] * (2 + len(pieces)),
        out_specs=VMEM_SPEC,
        scratch_shapes=[pltpu.VMEM(q.shape, jnp.bfloat16)],
        compiler_params=pltpu.CompilerParams(vmem_limit_bytes=MID_VMEM),
        cost_estimate=pl.CostEstimate(
            flops=1300000000, bytes_accessed=4000000, transcendentals=2500000
        ),
    )(info, q, to, *pieces)


def per_device(
    clip_store,
    text_tokens,
    candidates,
    clip_slot,
    text_positions,
    block_order,
    w_query,
    b_query,
    key_value_weight,
    value_offset_bias,
):
    me = lax.axis_index("ctx")
    plane = lax.axis_index("mp")
    group, member = me // MEMBERS, me % MEMBERS
    core = member % 2
    clips_here, clip_len, feat = clip_store.shape
    seqs, cands = candidates.shape
    text_len = text_positions.shape[1]
    width = w_query.shape[1]
    heads = width // HEAD

    sent = pack(candidates, clip_slot, me, clip_store, text_tokens)
    sent = lax.all_to_all(sent, "ctx", 0, 0, tiled=True)

    kv_flat = key_value_weight.reshape(key_value_weight.shape[0], -1)
    opposite = (plane + PLANES // 2) % PLANES
    kv_opposite = lax.dynamic_slice_in_dim(kv_flat, opposite * feat, feat, 0)
    text_at = lax.dynamic_index_in_dim(
        lax.dynamic_index_in_dim(text_positions, group, 0, keepdims=False).reshape(-1, MEMBERS),
        member, 1, keepdims=False,
    )
    clip_idx = STEP * jnp.arange(cands)[:, None] + jnp.arange(PART)[None, :]

    def clip_pos(dy):
        y = (group - dy) % GROUPS
        return (MEMBERS * (clip_idx + PART * y) + member).astype(jnp.int32).reshape(-1)

    cosine, sine = rope_tables(jnp.concatenate([text_at] + [clip_pos(dy) for dy in range(GROUPS)]))
    blocks = block_order.shape[0]
    block_len = (cands * clip_len + text_len) // blocks
    sub = block_len // MEMBERS
    send_from = sub * block_order.reshape(DEVICES, 1, 2) + jnp.arange(sub).reshape(1, sub, 1)
    send_from = send_from.astype(jnp.int32).reshape(-1, 1)
    sent, kv_flat, kv_opposite, cosine, sine, send_from = lax.optimization_barrier(
        (sent, kv_flat, kv_opposite, cosine, sine, send_from)
    )

    first, *others = unpack(candidates, clip_slot, group, sent, clips_here)
    arrived = [
        lax.ppermute(out, "ctx", ctx_pairs(lambda y, x, c, dy=dy: (y + dy, x, c)))
        for dy, out in enumerate(others, 1)
    ]
    first, arrived[1] = lax.optimization_barrier((first, arrived[1]))
    own = [first, jnp.concatenate(arrived, 0)]

    fwd, bwd = list(own), list(own)
    sums, parts, owners = None, [own], [plane]
    for hop in range(1, PLANES // 2):
        for h in range(len(own)):
            fwd[h] = lax.ppermute(fwd[h], "mp", shifted(PLANES, 1))
            bwd[h] = lax.ppermute(bwd[h], "mp", shifted(PLANES, -1))
        if hop in MULTIPLY_AT:
            sums = add_products(sums, parts, owners, w_query, kv_flat)
            fwd[-1], bwd[-1], sums = lax.optimization_barrier((fwd[-1], bwd[-1], sums))
            parts, owners = [], []
        parts += [list(fwd), list(bwd)]
        owners += [(plane - hop) % PLANES, (plane + hop) % PLANES]
    far = [
        lax.ppermute(jnp.where(core == 0, fwd[h], bwd[h]), ("ctx", "mp"), far_pairs())
        for h in range(len(own))
    ]
    sums = add_products(sums, parts, owners, w_query, kv_flat)
    far[-1], sums = lax.optimization_barrier((far[-1], sums))
    kv = finish_keys(sums[1], far, kv_opposite, cosine, sine, value_offset_bias)
    q = finish_queries(sums[0], far, opposite, w_query, cosine, sine, b_query)

    below = lax.ppermute(kv, "ctx", ctx_pairs(lambda y, x, c: (y, x + 1, c)))
    above = lax.ppermute(kv, "ctx", ctx_pairs(lambda y, x, c: (y, x - 1, c)))
    swap = ctx_pairs(lambda y, x, c: (y, x, 1 - c))
    beside = lax.ppermute(kv, "ctx", swap)
    above, q = lax.optimization_barrier((above, q))
    beyond = lax.ppermute(
        jnp.where(core == 0, above, below), "ctx",
        ctx_pairs(lambda y, x, c: (y, x + (-1 if c == 0 else 1), c)),
    )
    pieces = [kv, beside]
    for piece in (below, above, beyond):
        pieces += [piece, lax.ppermute(piece, "ctx", swap)]

    info = jnp.stack([group, member]).astype(jnp.int32)
    out = attend(info, q, send_from, pieces, heads, cands)

    send = out.reshape(DEVICES, sub, 2, width)
    recv = lax.all_to_all(send, "ctx", 0, 0, tiled=True)
    recv = recv.reshape(GROUPS, MEMBERS, sub, 2, width)
    return recv.transpose(0, 3, 2, 1, 4).reshape(seqs, 2, block_len, width)


def solution(mesh):
    placed = (
        P("ctx", None, "mp"),
        P(None, "ctx", "mp"),
        P(),
        P(),
        P(),
        P(),
        P(None, "mp"),
        P("mp"),
        P(None, None, "mp"),
        P("mp"),
    )
    return jax.shard_map(
        per_device,
        mesh=mesh,
        in_specs=placed,
        out_specs=P(None, "ctx", None, "mp"),
        check_vma=False,
    )
```
